256 devices in a mesh: trace: 64 (over z, x, core), freq: 4 (over y).
Axes of the slice: x: 4, y: 4, z: 8, core: 2. Of those that a mesh axis runs over, the one named last changes fastest.
Arguments:
- traces: float32 [32768, 2048], P('trace'), may hold values from -40 to 40, as said below
- shot_local: int32 [64, 512], P('trace'), may hold values from 0 to 15, never falling along the last dimension, each value on 1 to 64 neighbouring positions
- rec_slot: int32 [64, 512], P('trace'), may hold values from 0 to 255, as said below
- slot_station: int32 [64, 256], P('trace'), may hold values from 0 to 31, as said below
- cmp_owner: int32 [32768, 1], P('trace'), may hold values from 0 to 63; in each aligned block of 512 rows (0 to 511, 512 to 1023, ...) at most 16 rows name the same one
- cmp_local: int32 [32768], P('trace'), may hold values from 0 to 31
Outputs:
- shot_terms: float32 [1024, 1024], P('trace', 'freq')
- receiver_terms: float32 [2048, 1024], P('trace', 'freq')
- cmp_stack: float32 [2048, 2, 1024], P('trace', None, 'freq')
The draws below stay inside these ranges and needn't reach their ends.
Inputs may be any that keep to these rules, and one draw needn't show every extreme that they name: `shot_local`: every trace of every index of trace falls in one of its 16 shots, and every shot has a trace. `rec_slot`: slot s of an index of trace goes to the owner s // 4; on every index of trace, each slot is used by at least one trace. `slot_station`: the 4 slots of one index of trace towards one owner name distinct stations; every station of every owner is named by some slot. `cmp_owner`: at most 16 traces of one index of trace name the same owner. `traces`: samples lie within the range.
All inputs are finite; a program needn't handle non-finite values.
Results may differ from the reference program's by a relative error of at most 0.0001.
Values sent between devices are 32-bit elements; how exact they have to be, the bound alone decides.
A program may use at most 64 MiB of HBM per device.

```python
import math
import jax
import jax.numpy as jnp
import numpy as np
from jax import lax

NT = 2048
TDEV = 512
SWEEPS = 2
NF = 1024
SHOT_DEV = 16
REC_DEV = 32
CMP_DEV = 32
CAP = 4
CAPC = 16
TRACES = 32768
SHOTS = 1024
RECS = 2048
CMPS = 2048
N_TRACE = 64


def make_tone(key, amp_lo, amp_hi):
    key_freq, key_phase, key_amp = jax.random.split(key, 3)
    samples = jnp.arange(NT, dtype=jnp.int32)
    freq_bin = jax.random.randint(key_freq, (TRACES, 1), 1, max(2, NT // 8))
    phase = jax.random.randint(key_phase, (TRACES, 1), 0, NT)
    position = (freq_bin * samples[None, :] + phase) % NT
    amplitude = jnp.exp(jax.random.uniform(key_amp, (TRACES, 1), jnp.float32, jnp.log(amp_lo), jnp.log(amp_hi)))
    return amplitude * jnp.cos(2.0 * jnp.pi * position.astype(jnp.float32) / NT)


def draw_traces(key, part):
    key = jax.random.fold_in(key, 11)
    key_noise, key_one = jax.random.split(key, 2)
    noise = jnp.clip(jax.random.normal(key_noise, (TRACES, NT), jnp.float32), -8.0, 8.0)
    result = noise + make_tone(key_one, 1.0, 4.0)
    return result.astype(jnp.float32)


def draw_rec_slot(key, part):
    key = jax.random.fold_in(key, 12)
    slot_total = N_TRACE * CAP

    def one_row(row_key):
        key_extra, key_order = jax.random.split(row_key)
        extra = jax.random.randint(key_extra, (TDEV - slot_total,), 0, slot_total)
        whole = jnp.concatenate([jnp.arange(slot_total, dtype=jnp.int32), extra.astype(jnp.int32)])
        return jax.random.permutation(key_order, whole)
    return jax.vmap(one_row)(jax.random.split(key, N_TRACE)).astype(jnp.int32)


def draw_slot_station(key, part):
    key = jax.random.fold_in(key, 13)
    orders = jax.vmap(lambda row_key: jax.random.permutation(row_key, REC_DEV))(jax.random.split(key, N_TRACE))
    period = max(1, REC_DEV // CAP)
    sender = jnp.arange(N_TRACE, dtype=jnp.int32)[:, None, None]
    within = jnp.arange(CAP, dtype=jnp.int32)[None, None, :]
    position = (sender * CAP + within + sender // period) % REC_DEV
    owner = jnp.arange(N_TRACE, dtype=jnp.int32)[None, :, None]
    chosen = orders[owner, position]
    return chosen.reshape(N_TRACE, N_TRACE * CAP).astype(jnp.int32)


def plant(array, own_key, smallest, largest):
    longest = array.shape.index(max(array.shape))
    spots = []
    for shift in (0, 1):
        where = [jax.random.randint(jax.random.fold_in(own_key, axis), (), 0, length) for axis, length in enumerate(array.shape)]
        where[longest] = (where[longest] + shift) % array.shape[longest]
        spots.append(tuple(where))
    return array.at[spots[0]].set(smallest).at[spots[1]].set(largest)


def profile(count, total, most, slope):
    loads = [(1 << 20) // math.isqrt(grade ** slope) + 1 for grade in range(2, count + 1)]
    surplus, counts = total - most - (count - 1), [1] * (count - 1)
    while surplus > 0:
        free = [i for i in range(count - 1) if counts[i] < most]
        whole, left = sum([loads[i] for i in free]), surplus
        for i in free:
            more = min(most - counts[i], max(1, left * loads[i] // whole), surplus)
            counts[i] = counts[i] + more
            surplus = surplus - more
    return np.array([most] + counts)


def uneven(own_key, number_of, total, most, skew):
    if number_of == 2:
        one = jax.random.randint(own_key, (), max(1, total - most), min(most, total - 1) + 1)
        return jnp.stack([one, total - one])
    sizes = jnp.asarray(profile(number_of, total, most, skew), jnp.int32)
    twos = (number_of - 1) // 2
    source_of, sink = sizes[1:1 + 2 * twos:2], sizes[2:2 + 2 * twos:2]
    slack = jnp.minimum(source_of - 1, most - sink)
    passed = jax.random.randint(jax.random.fold_in(own_key, 1), (twos,), 0, 1 << 20) % (slack + 1)
    sizes = sizes.at[1:1 + 2 * twos:2].set(source_of - passed).at[2:2 + 2 * twos:2].set(sink + passed)
    return sizes[jax.random.permutation(jax.random.fold_in(own_key, 2), number_of)]


def routed_block(stream_key, own, number, rows, amount, top, bound, skew):
    sequence = jax.random.permutation(stream_key, amount)
    packed, usual = load_shares(amount, rows * top, bound, skew, True), load_shares(amount, rows * top, bound, skew, False)
    places = jnp.arange(amount)

    def named(tallies, offset_by):
        used = int((tallies > 0).sum())
        fixed = max(1, used // 4)
        shifted = fixed + (places - fixed + offset_by * (used - fixed)) % max(1, amount - fixed)
        return jnp.zeros((amount,), jnp.int32).at[sequence[jnp.where(places < fixed, places, shifted)]].set(jnp.asarray(tallies, jnp.int32))

    tallies = jnp.where(number % 4 == 0, named(packed, number // 4), named(usual, number - number // 4 - 1))
    mixed = jax.random.permutation(jax.random.fold_in(own, 3), amount)
    source_of, receiver = mixed[0:amount // 2 * 2:2], mixed[1:amount // 2 * 2:2]
    slack = jnp.minimum(tallies[source_of] - 1, bound - tallies[receiver]) // 2
    slack = jnp.where((source_of == sequence[0]) | (receiver == sequence[0]) | (tallies[receiver] == 0), 0, jnp.maximum(slack, 0))
    shifted = jax.random.randint(jax.random.fold_in(own, 4), (amount // 2,), 0, 1 << 20) % (slack + 1)
    tallies = tallies.at[source_of].add(-shifted).at[receiver].add(shifted)
    items = jnp.searchsorted(jnp.cumsum(tallies), jnp.arange(rows * top), side="right").astype(jnp.int32)
    grid = items.reshape(top, rows).T
    grid = grid[jax.random.permutation(jax.random.fold_in(own, 1), rows)]
    offset_by = jax.random.randint(jax.random.fold_in(own, 2), (rows, 1), 0, top)
    return jnp.take_along_axis(grid, (jnp.arange(top)[None, :] + offset_by) % top, axis=1)


def load_shares(count, total, limit, skew, full):
    loads = [(1 << 20) // math.isqrt(grade ** skew) + 1 for grade in range(1, count + 1)]
    largest = limit if full else min(limit, max(-(-total // count), total * loads[0] // sum(loads)))
    least = 1 if total - largest >= count - 1 else 0
    given, surplus = [largest] + [least] * (count - 1), total - largest - least * (count - 1)
    while surplus > 0:
        free = [i for i in range(1, count) if given[i] < largest] or [i for i in range(1, count) if given[i] < limit]
        mass, budget = sum([loads[i] for i in free]), surplus
        for i in free:
            addition = min(limit - given[i], max(1, budget * loads[i] // mass), surplus)
            given[i] = given[i] + addition
            surplus = surplus - addition
    return np.array(given)


def setup_inputs(seed: int = 0) -> dict:
    splits = jax.random.split(jax.random.key(seed), 7)
    traces = draw_traces(jax.random.fold_in(splits[6], 71), 0)
    shot_local = jax.vmap(lambda own: jnp.searchsorted(jnp.cumsum(uneven(own, SHOT_DEV, TDEV, 2 * TDEV // SHOT_DEV, 1)), jnp.arange(TDEV), side="right"))(jax.random.split(splits[1], N_TRACE)).reshape((N_TRACE, TDEV)).astype(jnp.int32)
    rec_slot = draw_rec_slot(jax.random.fold_in(splits[6], 71), 0)
    slot_station = draw_slot_station(jax.random.fold_in(splits[6], 71), 0)
    cmp_owner_keys = jax.random.split(jax.random.fold_in(splits[4], 1), TRACES // TDEV)
    cmp_owner_turns = jax.random.permutation(jax.random.fold_in(splits[4], 3), TRACES // TDEV)
    cmp_owner = jax.vmap(lambda own, number: routed_block(jax.random.fold_in(splits[4], 2), own, number, TDEV, N_TRACE, 1, CAPC, 2))(cmp_owner_keys, cmp_owner_turns).reshape((TRACES, 1))
    cmp_local = plant(jax.random.randint(splits[5], (TRACES,), 0, CMP_DEV), jax.random.fold_in(splits[5], 1), 0, CMP_DEV - 1).astype(jnp.int32)
    return {"traces": traces, "shot_local": shot_local, "rec_slot": rec_slot, "slot_station": slot_station, "cmp_owner": cmp_owner, "cmp_local": cmp_local}


def reference(traces, shot_local, rec_slot, slot_station, cmp_owner, cmp_local):
    spectrum = jnp.fft.rfft(traces, axis=1)[:, :NF]
    norm_factor = 1.0 / jnp.sqrt(jnp.float32(NT))
    real_part = (jnp.real(spectrum) * norm_factor).astype(jnp.float32)
    imag_part = (jnp.imag(spectrum) * norm_factor).astype(jnp.float32)
    power = real_part * real_part + imag_part * imag_part
    level = lax.optimization_barrier(jnp.mean(power, axis=1, keepdims=True))
    logs = jnp.log(power + 0.01 * level)
    device_of = (jnp.arange(TRACES) // TDEV).astype(jnp.int32)
    shot_g = (device_of * SHOT_DEV + shot_local.reshape(-1)).astype(jnp.int32)
    station = jnp.take_along_axis(slot_station, rec_slot, axis=1)
    rec_g = (rec_slot // CAP * REC_DEV + station).reshape(-1).astype(jnp.int32)
    cmp_g = (cmp_owner[:, 0] * CMP_DEV + cmp_local).astype(jnp.int32)
    ones = jnp.ones((TRACES,), jnp.float32)
    shot_count = jax.ops.segment_sum(ones, shot_g, num_segments=SHOTS)
    rec_count = jax.ops.segment_sum(ones, rec_g, num_segments=RECS)
    rec_trace = jnp.zeros_like(logs)
    shot_terms = jnp.zeros((SHOTS, NF), jnp.float32)
    receiver_terms = jnp.zeros((RECS, NF), jnp.float32)
    for sweep in range(SWEEPS):
        shot_terms = jax.ops.segment_sum(logs - rec_trace, shot_g, num_segments=SHOTS) / shot_count[:, None]
        shot_trace = shot_terms[shot_g]
        receiver_terms = jax.ops.segment_sum(logs - shot_trace, rec_g, num_segments=RECS) / rec_count[:, None]
        rec_trace = receiver_terms[rec_g]
    model = shot_trace + rec_trace
    expmodel = jnp.exp(model)
    mean_model = lax.optimization_barrier(jnp.mean(expmodel, axis=1, keepdims=True))
    wiener = jnp.exp(0.5 * model) / (expmodel + 0.3 * mean_model)
    decon = jnp.stack([wiener * real_part, wiener * imag_part], axis=1)
    cmp_stack = 0.25 * jax.ops.segment_sum(decon, cmp_g, num_segments=CMPS)
    return (shot_terms, receiver_terms, cmp_stack)
```

```python
import functools

import jax
import jax.numpy as jnp
import numpy as np
from jax import lax
from jax.experimental import pallas as pl
from jax.experimental.pallas import tpu as pltpu
from jax.sharding import PartitionSpec as P

NT = 2048
HALF = 1024
NB = 128
TDEV = 512
ROWS = 512
F32 = jnp.float32
BF16 = jnp.bfloat16
NT_DIMS = (((1,), (1,)), ((), ()))
TN_DIMS = (((0,), (0,)), ((), ()))


def twiddles():
    bins = np.arange(4)[:, None, None] * 256 + np.arange(2)[None, :, None] + 2 * np.arange(NB)[None, None, :]
    low = -2.0 * np.pi * ((np.arange(128)[:, None] * bins[:, :, None, :]) % NT) / NT
    high = -2.0 * np.pi * ((128 * np.arange(8)[:, None] * bins[:, :, None, :]) % NT) / NT
    norm = NT**-0.5
    low = np.concatenate([np.cos(low), np.sin(low)], axis=-1) * norm
    high = np.concatenate([np.cos(high), np.sin(high)], axis=-1)
    return low.astype(np.float32), high.astype(np.float32)


def split(x, parts):
    out = []
    for i in range(parts):
        piece = x.astype(BF16)
        out.append(piece)
        if i + 1 < parts:
            x = x - piece.astype(F32)
    return out


def hot_dot(hot, x, parts=3, dims=(((1,), (0,)), ((), ()))):
    n = x.shape[1]
    full = lax.dot_general(hot, jnp.concatenate(split(x, parts), axis=1), dims, preferred_element_type=F32)
    total = full[:, :n]
    for i in range(1, parts):
        total = total + full[:, i * n:(i + 1) * n]
    return total


def iota(shape, axis):
    return lax.broadcasted_iota(jnp.int32, shape, axis)


def hot(condition):
    return jnp.where(condition, 1.0, 0.0).astype(BF16)


def kernel(
    traces, index, low_tab, high_tab,
    shot_out, rec_out, cmp_out,
    xbuf, low, high, table, uhi, ulo, vhi, vlo, level, spec, logs,
    slot_rows, slot_cols, shot_rows, shot_cols, cmp_hot, owner_cols,
    meta_send, meta_recv, sum_send, sum_recv, term_send, term_recv, q_send, q_recv,
    dense, rs0, rs1, rs2, rs3,
    x_sem, tab_sem, a2a_send, a2a_recv, q_ssem, q_rsem, rs_send, rs0_sem, rs1_sem, rs2_sem, rs3_sem,
):
    me = lax.axis_index("trace")
    band = lax.axis_index("freq")
    z = lax.div(me, 8)
    x = lax.rem(lax.div(me, 2), 4)
    core = lax.rem(me, 2)

    barrier = pltpu.get_barrier_semaphore()

    @pl.loop(1, 64)
    def _(p):
        pl.semaphore_signal(barrier, inc=1, device_id={"trace": lax.rem(me + p, 64)})

    for p in range(1, 4):
        pl.semaphore_signal(barrier, inc=1, device_id={"freq": lax.rem(band + p, 4)})

    def x_copy(c):
        rows = pl.ds(c * 64, 64)
        return pltpu.make_async_copy(traces.at[rows], xbuf.at[rows], x_sem.at[c])

    low_copy = pltpu.make_async_copy(low_tab.at[band], low, tab_sem.at[0])
    high_copy = pltpu.make_async_copy(high_tab.at[band], high, tab_sem.at[1])
    low_copy.start()
    high_copy.start()
    for c in range(8):
        x_copy(c).start()

    by_lane = index[...]
    by_row = jnp.transpose(by_lane)
    shot_lane, slot_lane, cmp_lane, station_lane = (by_lane[i:i + 1, :] for i in range(4))
    shot_row, slot_row = by_row[:, 0:1], by_row[:, 1:2]

    i0 = iota((ROWS, TDEV), 0)
    slot_of = (lax.shift_right_logical(i0, 3) * 4 + (i0 & 3)).astype(F32)
    half_of = lax.shift_right_logical(i0, 2) & 1
    same = slot_of == slot_lane
    for h in range(2):
        slot_rows[:, h * TDEV:(h + 1) * TDEV] = hot(same & (half_of == h))
    count = jnp.sum(jnp.where(same, 1.0, 0.0), axis=1, keepdims=True)
    station = jnp.sum(jnp.where(slot_of == iota((ROWS, TDEV), 1).astype(F32), station_lane, 0.0), axis=1, keepdims=True)
    meta_send[...] = jnp.where(iota((ROWS, NB), 1) < 64, station, count)

    i1 = iota((TDEV, ROWS), 1)
    slot_of = (lax.shift_right_logical(i1, 3) * 4 + (i1 & 3)).astype(F32)
    half_of = lax.shift_right_logical(i1, 2) & 1
    same = slot_of == slot_row
    for h in range(2):
        slot_cols[h * TDEV:(h + 1) * TDEV, :] = hot(same & (half_of == h))

    j0, j1 = iota((32, TDEV), 0).astype(F32), iota((TDEV, 32), 1).astype(F32)
    for h in range(2):
        shot_rows[:, h * TDEV:(h + 1) * TDEV] = hot(j0 == shot_lane + 16.0 * h)
        shot_cols[h * TDEV:(h + 1) * TDEV, :] = hot(j1 == shot_row + 16.0 * h)

    def exchange(phase, source, target):
        mine = pl.ds(pl.multiple_of(me * 8, 8), 8)
        target[mine, :] = source[mine, :]

        @pl.loop(1, 64)
        def _(p):
            other = lax.rem(me + p, 64)
            pltpu.make_async_remote_copy(
                src_ref=source.at[pl.ds(pl.multiple_of(other * 8, 8), 8)],
                dst_ref=target.at[mine],
                send_sem=a2a_send.at[phase],
                recv_sem=a2a_recv.at[phase],
                device_id={"trace": other},
            ).start()

    def arrived(phase, target):
        rows = pl.ds(0, 504)
        pltpu.make_async_copy(target.at[rows], target.at[rows], a2a_recv.at[phase]).wait()

    def sent(phase, source):
        rows = pl.ds(0, 504)
        pltpu.make_async_copy(source.at[rows], source.at[rows], a2a_send.at[phase]).wait()

    pl.semaphore_wait(barrier, 66)
    exchange(0, meta_send, meta_recv)

    low_copy.wait()
    high_copy.wait()
    for h in range(2):
        low_re, low_im = low[h, :, :NB], low[h, :, NB:]
        for n1 in range(8):
            high_re, high_im = high[h, n1:n1 + 1, :NB], high[h, n1:n1 + 1, NB:]
            re_hi, re_lo = split(low_re * high_re - low_im * high_im, 2)
            im_hi, im_lo = split(low_re * high_im + low_im * high_re, 2)
            table[h, n1 * 128:(n1 + 1) * 128, :] = jnp.concatenate([re_hi, im_hi, re_lo, im_lo], axis=1)

    sign = 1.0 - 2.0 * (iota((1, HALF), 1) & 1).astype(F32)
    for part in range(2):
        @pl.loop(0, 4)
        def _(b):
            c = part * 4 + b
            x_copy(c).wait()
            rows = pl.ds(pl.multiple_of(c * 64, 64), 64)
            first, second = xbuf[rows, :HALF], xbuf[rows, HALF:]
            u, v = first + second, first - second
            nyquist = jnp.sum(u * sign, axis=1, keepdims=True) * (1.0 / HALF)
            rest = u - nyquist * sign
            energy = jnp.sum(rest * rest + v * v, axis=1, keepdims=True) * 0.5
            mean = jnp.sum(u, axis=1, keepdims=True)
            level[rows, :] = jnp.broadcast_to((energy + mean * mean * (1.0 / NT)) * (0.5 / 1024.0), (64, NB))
            uhi[rows, :], ulo[rows, :] = split(u, 2)
            vhi[rows, :], vlo[rows, :] = split(v, 2)

        rows = slice(part * 256, (part + 1) * 256)
        floor = 0.01 * level[rows, :]
        for h, (hi, lo) in enumerate(((uhi, ulo), (vhi, vlo))):
            full = jnp.dot(hi[rows, :], table[h], preferred_element_type=F32)
            rest = jnp.dot(lo[rows, :], table[h, :, :256], preferred_element_type=F32)
            both = full[:, :256] + (full[:, 256:] + rest)
            spec[rows, h * 256:(h + 1) * 256] = both
            re, im = both[:, :NB], both[:, NB:]
            logs[h * TDEV + part * 256:h * TDEV + (part + 1) * 256, :] = jnp.log(re * re + im * im + floor)

    shots, slots = shot_rows[...], slot_rows[...]
    shot_count = jnp.sum(shots.astype(F32), axis=1, keepdims=True)
    counts = lax.dot_general(shots, slots, NT_DIMS, preferred_element_type=F32).astype(BF16)
    counts_t = lax.dot_general(slots, shots, NT_DIMS, preferred_element_type=F32).astype(BF16)
    shot_sums = hot_dot(shots, logs[...])
    slot_sums = hot_dot(slots, logs[...])

    shot_terms = shot_sums / shot_count
    sum_send[0] = slot_sums - hot_dot(counts_t, shot_terms)
    exchange(1, sum_send.at[0], sum_recv.at[0])

    arrived(0, meta_recv)
    stations = meta_recv[:, 0:64]
    k1 = iota((ROWS, 64), 1)
    k0 = lax.shift_right_logical(iota((ROWS, 64), 0), 2) & 1
    owner_cols[...] = hot((stations == (k1 & 31).astype(F32)) & (k0 == lax.shift_right_logical(k1, 5)))
    owner = owner_cols[...]
    incoming = jnp.broadcast_to(meta_recv[:, 64:65], (ROWS, NB))
    station_count = hot_dot(owner, incoming, 2, TN_DIMS)

    for c in range(8):
        rows = slice(c * 256, (c + 1) * 256)
        cmp_hot[rows, :] = hot((iota((256, TDEV), 0) + c * 256).astype(F32) == cmp_lane)

    for sweep in range(2):
        arrived(1 + 2 * sweep, sum_recv.at[sweep])
        terms = hot_dot(owner, sum_recv[sweep], 3, TN_DIMS) / station_count
        term_send[sweep] = hot_dot(owner, terms)
        exchange(2 + 2 * sweep, term_send.at[sweep], term_recv.at[sweep])
        if sweep == 0:
            arrived(2, term_recv.at[0])
            shot_terms = (shot_sums - hot_dot(counts, term_recv[0])) / shot_count
            sum_send[1] = slot_sums - hot_dot(counts_t, shot_terms)
            exchange(3, sum_send.at[1], sum_recv.at[1])
    rec_out[...] = terms
    shot_out[...] = shot_terms
    shot_part = hot_dot(shot_cols[...], shot_terms)
    arrived(4, term_recv.at[1])
    model = shot_part + hot_dot(slot_cols[...], term_recv[1])
    root = jnp.exp(0.5 * model)
    logs[...] = root
    both = root[:TDEV] * root[:TDEV] + root[TDEV:] * root[TDEV:]
    ones = jnp.ones((8, NB), BF16)
    partial = jnp.zeros((8, TDEV), F32)
    for piece in split(both, 3):
        partial = partial + lax.dot_general(ones, piece, NT_DIMS, preferred_element_type=F32)
    q_send[...] = partial
    q_recv[band] = partial
    q_copies = []
    for p in range(1, 4):
        copy = pltpu.make_async_remote_copy(
            src_ref=q_send, dst_ref=q_recv.at[band], send_sem=q_ssem.at[p - 1], recv_sem=q_rsem.at[p - 1],
            device_id={"freq": lax.rem(band + p, 4)},
        )
        copy.start()
        q_copies.append(copy)
    for copy in q_copies:
        copy.wait()
    total = (q_recv[0] + q_recv[1]) + (q_recv[2] + q_recv[3])
    floor = jnp.broadcast_to(jnp.transpose(total)[:, 0:1], (TDEV, NB)) * (0.3 / 1024.0)
    for h in range(2):
        root = logs[h * TDEV:(h + 1) * TDEV, :]
        wiener = root / (root * root + floor)
        for c in range(2):
            cols = slice((2 * h + c) * NB, (2 * h + c + 1) * NB)
            spec[:, cols] = wiener * spec[:, cols]

    other_half = pl.ds(pl.multiple_of((1 - core) * 1024, 1024), 1024)
    own_half = pl.ds(pl.multiple_of(core * 1024, 1024), 1024)

    def stack(g, half):
        parts = jnp.concatenate(split(spec[:, g * NB:(g + 1) * NB], 2), axis=1)
        full = jnp.dot(cmp_hot[half, :], parts, preferred_element_type=F32)
        return full[:, :NB] + full[:, NB:]

    sibling = {"trace": me + 1 - 2 * core}

    def at_x(step):
        return {"trace": z * 8 + lax.rem(x + step, 4) * 2 + core}

    def x_rows(step, first, size):
        return pl.ds(pl.multiple_of(core * 1024 + lax.rem(x + step, 4) * 256 + first, 128), size)

    def send(src, dst, stage, sem, to):
        return pltpu.make_async_remote_copy(
            src_ref=src, dst_ref=dst, send_sem=rs_send.at[stage], recv_sem=sem, device_id=to
        )

    def step0(g):
        return send(dense.at[g, other_half], rs0.at[g], 0, rs0_sem.at[g], sibling)

    def step1(g, d):
        return send(dense.at[g, x_rows(2, 128 * d, 128)], rs1.at[g, d], 1, rs1_sem.at[g, d], at_x(1 + 2 * d))

    def step2(g, d):
        return send(dense.at[g, x_rows(1 + 2 * d, 0, 256)], rs2.at[g, d], 2, rs2_sem.at[g, d], at_x(1 + 2 * d))

    def begin(g):
        dense[g, other_half, :] = stack(g, other_half)
        step0(g).start()
        dense[g, own_half, :] = stack(g, own_half)

    def after0(g):
        step0(g).wait_recv()
        dense[g, own_half, :] = dense[g, own_half, :] + rs0[g]
        for d in range(2):
            step1(g, d).start()

    def after1(g):
        for d in range(2):
            step1(g, d).wait_recv()
            rows = x_rows(1 + 2 * d, 128 * d, 128)
            dense[g, rows, :] = dense[g, rows, :] + rs1[g, d]
            step2(g, d).start()

    def after2(g):
        mine = x_rows(0, 0, 256)
        for d in range(2):
            step2(g, d).wait_recv()
        dense[g, mine, :] = dense[g, mine, :] + (rs2[g, 0] + rs2[g, 1])
        own = pl.ds(pl.multiple_of(z * 32, 32), 32)
        first = pl.multiple_of(core * 1024 + x * 256, 256)
        rs3[g, own, :] = dense[g, pl.ds(first + z * 32, 32), :]

        @pl.loop(1, 8)
        def _(p):
            there = lax.rem(z + p, 8)
            send(
                dense.at[g, pl.ds(pl.multiple_of(first + there * 32, 32), 32)], rs3.at[g, own],
                3, rs3_sem.at[g], {"trace": there * 8 + x * 2 + core},
            ).start()

    def after3(g):
        rows = pl.ds(0, 224)
        pltpu.make_async_copy(rs3.at[g, rows], rs3.at[g, rows], rs3_sem.at[g]).wait()
        total = rs3[g, 0:32, :]
        for s in range(1, 8):
            total = total + rs3[g, s * 32:(s + 1) * 32, :]
        cmp_out[g] = 0.25 * total

    for step in range(8):
        for offset, stage in ((0, begin), (1, after0), (2, after1), (3, after2), (4, after3)):
            if 0 <= step - offset < 4:
                stage(step - offset)

    sent(0, meta_send)
    for sweep in range(2):
        sent(1 + 2 * sweep, sum_send.at[sweep])
        sent(2 + 2 * sweep, term_send.at[sweep])
    for stage, ref in (
        (0, dense.at[:, pl.ds(0, 1024)]), (1, dense.at[:, pl.ds(0, 256)]),
        (2, dense.at[:, pl.ds(0, 512)]), (3, dense.at[:, pl.ds(0, 224)]),
    ):
        pltpu.make_async_copy(ref, ref, rs_send.at[stage]).wait()


def shards(low_tab, high_tab, traces, shot_local, rec_slot, slot_station, cmp_owner, cmp_local):
    owner = cmp_owner[:, 0]
    row = (owner % 2) * 1024 + (owner // 2 % 4) * 256 + owner // 8 * 32 + cmp_local
    station = jnp.pad(slot_station, ((0, 0), (0, TDEV - slot_station.shape[1])))
    index = jnp.concatenate([shot_local, rec_slot, row[None, :], station], axis=0).astype(F32)
    index = jnp.concatenate([index, jnp.zeros((4, TDEV), F32)], axis=0)
    vmem = pltpu.VMEM
    dma = pltpu.SemaphoreType.DMA
    shot, rec, cmp = pl.pallas_call(
        kernel,
        out_shape=(
            jax.ShapeDtypeStruct((32, NB), F32),
            jax.ShapeDtypeStruct((64, NB), F32),
            jax.ShapeDtypeStruct((4, 32, NB), F32),
        ),
        in_specs=[
            pl.BlockSpec(memory_space=pl.ANY),
            pl.BlockSpec(memory_space=vmem),
            pl.BlockSpec(memory_space=pl.ANY),
            pl.BlockSpec(memory_space=pl.ANY),
        ],
        out_specs=(pl.BlockSpec(memory_space=vmem),) * 3,
        scratch_shapes=[
            vmem((TDEV, NT), F32), vmem((2, 128, 256), F32), vmem((2, 8, 256), F32), vmem((2, HALF, 512), BF16),
            vmem((TDEV, HALF), BF16), vmem((TDEV, HALF), BF16), vmem((TDEV, HALF), BF16), vmem((TDEV, HALF), BF16),
            vmem((TDEV, NB), F32), vmem((TDEV, 512), F32), vmem((2 * TDEV, NB), F32),
            vmem((ROWS, 2 * TDEV), BF16), vmem((2 * TDEV, ROWS), BF16),
            vmem((32, 2 * TDEV), BF16), vmem((2 * TDEV, 32), BF16),
            vmem((2048, TDEV), BF16), vmem((ROWS, 64), BF16),
            vmem((ROWS, NB), F32), vmem((ROWS, NB), F32),
            vmem((2, ROWS, NB), F32), vmem((2, ROWS, NB), F32), vmem((2, ROWS, NB), F32), vmem((2, ROWS, NB), F32),
            vmem((8, TDEV), F32), vmem((4, 8, TDEV), F32),
            vmem((4, 2048, NB), F32), vmem((4, 1024, NB), F32), vmem((4, 2, 128, NB), F32),
            vmem((4, 2, 256, NB), F32), vmem((4, 256, NB), F32),
            dma((8,)), dma((2,)), dma((5,)), dma((5,)), dma((3,)), dma((3,)),
            dma((4,)), dma((4,)), dma((4, 2)), dma((4, 2)), dma((4,)),
        ],
        compiler_params=pltpu.CompilerParams(
            collective_id=0, has_side_effects=True, vmem_limit_bytes=56 * 1024 * 1024
        ),
    )(traces, index, low_tab, high_tab)

    def interleave(a, b):
        return jnp.stack([a, b], axis=-1).reshape(a.shape[:-1] + (2 * NB,))

    return (
        interleave(shot[:16], shot[16:]),
        interleave(rec[:32], rec[32:]),
        interleave(jnp.stack([cmp[0], cmp[1]], axis=1), jnp.stack([cmp[2], cmp[3]], axis=1)),
    )


def solution(mesh):
    low, high = twiddles()
    body = jax.shard_map(
        shards,
        mesh=mesh,
        in_specs=(
            P(), P(),
            P("trace", None),
            P("trace", None),
            P("trace", None),
            P("trace", None),
            P("trace", None),
            P("trace"),
        ),
        out_specs=(P("trace", "freq"), P("trace", "freq"), P("trace", None, "freq")),
        check_vma=False,
    )
    return functools.partial(body, low, high)
```

```python
import functools

import jax
import jax.numpy as jnp
import numpy as np
from jax import lax
from jax.experimental import pallas as pl
from jax.experimental.pallas import tpu as pltpu
from jax.sharding import PartitionSpec as P

NT = 2048
HALF = 1024
NB = 128
TDEV = 512
SLOTS = 256
F32 = jnp.float32
BF16 = jnp.bfloat16
NT_DIMS = (((1,), (1,)), ((), ()))
TN_DIMS = (((0,), (0,)), ((), ()))


def twiddles():
    bins = np.arange(4)[:, None, None] * 256 + np.arange(2)[None, :, None] + 2 * np.arange(NB)[None, None, :]
    low = -2.0 * np.pi * ((np.arange(128)[:, None] * bins[:, :, None, :]) % NT) / NT
    high = -2.0 * np.pi * ((128 * np.arange(8)[:, None] * bins[:, :, None, :]) % NT) / NT
    norm = NT**-0.5
    low = np.concatenate([np.cos(low), np.sin(low)], axis=-1) * norm
    high = np.concatenate([np.cos(high), np.sin(high)], axis=-1)
    return low.astype(np.float32), high.astype(np.float32)


def split(x, parts):
    out = []
    for i in range(parts):
        piece = x.astype(BF16)
        out.append(piece)
        if i + 1 < parts:
            x = x - piece.astype(F32)
    return out


def hot_dot(hot, x, parts=3, dims=(((1,), (0,)), ((), ()))):
    n = x.shape[1]
    full = lax.dot_general(hot, jnp.concatenate(split(x, parts), axis=1), dims, preferred_element_type=F32)
    total = full[:, :n]
    for i in range(1, parts):
        total = total + full[:, i * n:(i + 1) * n]
    return total


def iota(shape, axis):
    return lax.broadcasted_iota(jnp.int32, shape, axis)


def hot(condition):
    return jnp.where(condition, 1.0, 0.0).astype(BF16)


def kernel(
    traces, shot_in, slot_in, station_in, owner_in, local_in, low_tab, high_tab,
    out,
    xbuf, low, high, table, uhi, ulo, vhi, vlo, level, spec, logs, roots,
    shot_idx, slot_idx, station_idx, owner_idx, local_idx,
    slot_rows, slot_cols, shot_cols, cmp_hot, owner_cols,
    first_send, first_recv, sum_send, sum_recv, term_send, term_recv, q_send, q_recv,
    dense, rs0, rs1, rs2, rs3, stacked,
    x_sem, tab_sem, idx_sem, a2a_send, a2a_recv, q_ssem, q_rsem, rs_send, rs0_sem, rs1_sem, rs2_sem, rs3_sem,
):
    me = lax.axis_index("trace")
    band = lax.axis_index("freq")
    z = lax.div(me, 8)
    x = lax.rem(lax.div(me, 2), 4)
    core = lax.rem(me, 2)
    pending = []

    def x_copy(c):
        rows = pl.ds(c * 64, 64)
        return pltpu.make_async_copy(traces.at[rows], xbuf.at[rows], x_sem.at[c])

    low_copy = pltpu.make_async_copy(low_tab.at[band], low, tab_sem.at[0])
    high_copy = pltpu.make_async_copy(high_tab.at[band], high, tab_sem.at[1])
    index_copies = [
        pltpu.make_async_copy(source, target, idx_sem.at[i])
        for i, (source, target) in enumerate((
            (shot_in, shot_idx), (slot_in, slot_idx), (station_in, station_idx), (owner_in, owner_idx), (local_in, local_idx),
        ))
    ]
    low_copy.start()
    high_copy.start()
    for c in range(8):
        x_copy(c).start()
    for copy in index_copies:
        copy.start()

    barrier = pltpu.get_barrier_semaphore()

    @pl.loop(1, 64)
    def _(p):
        pl.semaphore_signal(barrier, inc=1, device_id={"trace": lax.rem(me + p, 64)})

    for p in range(1, 4):
        pl.semaphore_signal(barrier, inc=1, device_id={"freq": lax.rem(band + p, 4)})

    def exchange(leg, source_of, target):
        sems = dict(send_sem=a2a_send.at[leg], recv_sem=a2a_recv.at[leg])

        def put(other):
            pltpu.make_async_remote_copy(
                src_ref=source_of(other), dst_ref=target(me), device_id={"trace": other}, **sems
            ).start()

        @pl.loop(0, 7)
        def _(k):
            side = 1 - 2 * lax.rem(k, 2)
            there = lax.rem(z + 12 + side * lax.div(k + 1, 2), 8) * 8
            for dx in (2, 1, 3, 0):
                for dc in (1, 0):
                    put(there + lax.rem(x + dx, 4) * 2 + lax.rem(core + dc, 2))

        for dx in (2, 1, 3, 0):
            for dc in (1, 0):
                if dx or dc:
                    put(z * 8 + lax.rem(x + dx, 4) * 2 + lax.rem(core + dc, 2))
        pltpu.make_async_copy(source_of(me), target(me), a2a_recv.at[leg]).start()

    def four(ref):
        return lambda d: ref.at[pl.ds(pl.multiple_of(d * 4, 4), 4)]

    def five(ref):
        return lambda d: ref.at[d, pl.ds(0, 5)]

    def exchange_rows(leg, source, target):
        exchange(leg, four(source), four(target))
        part = source.at[pl.ds(0, 252)]
        pending.append(pltpu.make_async_copy(part, part, a2a_send.at[leg]).wait)

    def arrived(leg, target):
        pltpu.make_async_copy(target, target, a2a_recv.at[leg]).wait()

    low_copy.wait()
    high_copy.wait()
    for h in range(2):
        low_re, low_im = low[h, :, :NB], low[h, :, NB:]
        for n1 in range(8):
            high_re, high_im = high[h, n1:n1 + 1, :NB], high[h, n1:n1 + 1, NB:]
            re_hi, re_lo = split(low_re * high_re - low_im * high_im, 2)
            im_hi, im_lo = split(low_re * high_im + low_im * high_re, 2)
            table[h, n1 * 128:(n1 + 1) * 128, :] = jnp.concatenate([re_hi, im_hi, re_lo, im_lo], axis=1)

    for copy in index_copies:
        copy.wait()
    shot_lane = shot_idx[...]
    slot_lane = slot_idx[...]
    station_lane = station_idx[...].astype(F32)
    slot_rows[...] = hot(iota((SLOTS, TDEV), 0) == slot_lane)
    shots = hot(iota((16, TDEV), 0) == shot_lane)
    slots = slot_rows[...]
    shot_count = jnp.sum(shots.astype(F32), axis=1, keepdims=True)
    counts = lax.dot_general(shots, slots, NT_DIMS, preferred_element_type=F32).astype(BF16)
    counts_t = lax.dot_general(slots, shots, NT_DIMS, preferred_element_type=F32).astype(BF16)
    slot_count = lax.dot_general(jnp.ones((8, TDEV), BF16), slots, NT_DIMS, preferred_element_type=F32)[0:1, :]
    meta = jnp.zeros((64, NB), F32)
    lane = iota((64, NB), 1)
    for c in range(4):
        named = iota((64, SLOTS), 1) == iota((64, SLOTS), 0) * 4 + c
        meta = jnp.where(lane == c, jnp.sum(jnp.where(named, station_lane, 0.0), axis=1, keepdims=True), meta)
        meta = jnp.where(lane == 4 + c, jnp.sum(jnp.where(named, slot_count, 0.0), axis=1, keepdims=True), meta)
    first_send[:, 4:5, :] = meta.reshape(64, 1, NB)

    sign = 1.0 - 2.0 * (iota((1, HALF), 1) & 1).astype(F32)

    @pl.loop(0, 8)
    def _(c):
        x_copy(c).wait()
        rows = pl.ds(pl.multiple_of(c * 64, 64), 64)
        first, second = xbuf[rows, :HALF], xbuf[rows, HALF:]
        u, v = first + second, first - second
        nyquist = jnp.sum(u * sign, axis=1, keepdims=True) * (1.0 / HALF)
        rest = u - nyquist * sign
        energy = jnp.sum(rest * rest + v * v, axis=1, keepdims=True) * 0.5
        mean = jnp.sum(u, axis=1, keepdims=True)
        level[rows, :] = jnp.broadcast_to((energy + mean * mean * (1.0 / NT)) * (0.01 * 0.5 / 1024.0), (64, NB))
        uhi[rows, :], ulo[rows, :] = split(u, 2)
        vhi[rows, :], vlo[rows, :] = split(v, 2)

    shot_sums, slot_sums, shot_terms = [None, None], [None, None], [None, None]
    for h, (hi, lo) in enumerate(((uhi, ulo), (vhi, vlo))):
        for part in range(2):
            rows = slice(part * 256, (part + 1) * 256)
            full = jnp.dot(hi[rows, :], table[h], preferred_element_type=F32)
            rest = jnp.dot(lo[rows, :], table[h, :, :256], preferred_element_type=F32)
            both = full[:, :256] + (full[:, 256:] + rest)
            spec[rows, h * 256:(h + 1) * 256] = both
            re, im = both[:, :NB], both[:, NB:]
            logs[h, rows, :] = jnp.log(re * re + im * im + level[rows, :])
        shot_sums[h] = hot_dot(shots, logs[h])
        slot_sums[h] = hot_dot(slot_rows[...], logs[h])
        shot_terms[h] = shot_sums[h] / shot_count
        sums = slot_sums[h] - hot_dot(counts_t, shot_terms[h])
        if h == 0:
            first_send[:, 0:4, :] = sums.reshape(64, 4, NB)
            pl.semaphore_wait(barrier, 66)
            exchange(0, five(first_send), five(first_recv))
            part = first_send.at[pl.ds(0, 63), pl.ds(0, 5)]
            pending.append(pltpu.make_async_copy(part, part, a2a_send.at[0]).wait)
        else:
            sum_send[0] = sums
            exchange_rows(1, sum_send.at[0], sum_recv.at[0])

    by_row = jnp.transpose(jnp.concatenate(
        [shot_lane.astype(F32), slot_lane.astype(F32), jnp.zeros((6, TDEV), F32)], axis=0
    ))
    shot_cols[...] = hot(iota((TDEV, 16), 1).astype(F32) == by_row[:, 0:1])
    slot_cols[...] = hot(iota((TDEV, SLOTS), 1).astype(F32) == by_row[:, 1:2])

    part = first_recv.at[:, pl.ds(0, 5)]
    pltpu.make_async_copy(part, part, a2a_recv.at[0]).wait()
    of_source = hot(lax.shift_right_logical(iota((SLOTS, 64), 0), 2) == iota((SLOTS, 64), 1))
    meta = hot_dot(of_source, first_recv[:, 4:5, :].reshape(64, NB), 2)
    lane, own = iota((SLOTS, NB), 1), iota((SLOTS, NB), 0) & 3
    station = jnp.sum(jnp.where(lane == own, meta, 0.0), axis=1, keepdims=True)
    count = jnp.sum(jnp.where(lane == own + 4, meta, 0.0), axis=1, keepdims=True)
    owner_cols[...] = hot(station == iota((SLOTS, 32), 1).astype(F32))
    owner = owner_cols[...]
    station_count = hot_dot(owner, jnp.broadcast_to(count, (SLOTS, NB)), 2, TN_DIMS)
    terms = [None, None]

    def at_owner(sweep, h):
        if sweep == 0 and h == 0:
            sums = first_recv[:, 0:4, :].reshape(SLOTS, NB)
        else:
            slot = sweep * 2 + h - 1
            arrived(1 if sweep == 0 else 4 + h, sum_recv.at[slot])
            sums = sum_recv[slot]
        terms[h] = hot_dot(owner, sums, 3, TN_DIMS) / station_count
        slot = sweep * 2 + h
        term_send[slot] = hot_dot(owner, terms[h])
        exchange_rows(2 + sweep * 4 + h, term_send.at[slot], term_recv.at[slot])

    def at_source(h):
        arrived(2 + h, term_recv.at[h])
        shot_terms[h] = (shot_sums[h] - hot_dot(counts, term_recv[h])) / shot_count
        sum_send[1 + h] = slot_sums[h] - hot_dot(counts_t, shot_terms[h])
        exchange_rows(4 + h, sum_send.at[1 + h], sum_recv.at[1 + h])

    at_owner(0, 0)
    at_owner(0, 1)
    for c in range(4):
        rows = slice(c * 512, (c + 1) * 512)
        owner_lane = owner_idx[...]
        local_lane = local_idx[...]
        place = (owner_lane & 1) * 1024 + lax.shift_right_logical(local_lane, 4) * 512 + (
            lax.shift_right_logical(owner_lane, 1) & 3) * 128 + lax.shift_right_logical(owner_lane, 3) * 16 + (local_lane & 15)
        cmp_hot[rows, :] = hot(iota((512, TDEV), 0) + c * 512 == place)
    at_source(0)
    at_source(1)
    at_owner(1, 0)
    at_owner(1, 1)

    k0, k1 = iota((256, 256), 0), iota((256, 256), 1)
    order = hot(k1 == 2 * (k0 & 127) + lax.shift_right_logical(k0, 7))

    def ordered(even, odd):
        total = jnp.zeros((even.shape[0], 256), F32)
        for piece in split(jnp.concatenate([even, odd], axis=1), 3):
            total = total + jnp.dot(piece, order, preferred_element_type=F32)
        return total

    out[0:16, :] = ordered(shot_terms[0], shot_terms[1])
    out[16:48, :] = ordered(terms[0], terms[1])
    shot_part = [hot_dot(shot_cols[...], shot_terms[h]) for h in range(2)]
    ones = jnp.ones((8, NB), BF16)
    partial = jnp.zeros((8, TDEV), F32)
    for h in range(2):
        arrived(6 + h, term_recv.at[2 + h])
        root = jnp.exp(0.5 * (shot_part[h] + hot_dot(slot_cols[...], term_recv[2 + h])))
        roots[h] = root
        for piece in split(root * root, 3):
            partial = partial + lax.dot_general(ones, piece, NT_DIMS, preferred_element_type=F32)
    q_send[...] = partial[0:1, :]
    q_recv[band] = partial[0:1, :]
    q_copies = []
    for p in (2, 1, 3):
        copy = pltpu.make_async_remote_copy(
            src_ref=q_send, dst_ref=q_recv.at[band], send_sem=q_ssem.at[p - 1], recv_sem=q_rsem.at[p - 1],
            device_id={"freq": lax.rem(band + p, 4)},
        )
        copy.start()
        q_copies.append(copy)
    for copy in q_copies:
        copy.wait()
    total = (q_recv[0] + q_recv[1]) + (q_recv[2] + q_recv[3])
    floor = jnp.transpose(jnp.broadcast_to(total, (8, TDEV)))[:, 0:1] * (0.3 / 1024.0)
    floor = jnp.broadcast_to(floor, (TDEV, NB))
    for h in range(2):
        root = roots[h]
        wiener = root / (root * root + floor)
        for c in range(2):
            cols = slice((2 * h + c) * NB, (2 * h + c + 1) * NB)
            spec[:, cols] = wiener * spec[:, cols]

    sibling = {"trace": me + 1 - 2 * core}

    def part_rows(of_core, c):
        return pl.ds(pl.multiple_of(of_core * 1024 + (c % 2) * 512, 512), 512)

    def stack(g, rows):
        parts = jnp.concatenate(split(spec[:, g * NB:(g + 1) * NB], 2), axis=1)
        full = jnp.dot(cmp_hot[rows, :], parts, preferred_element_type=F32)
        return full[:, :NB] + full[:, NB:]

    def at_x(step):
        return {"trace": z * 8 + lax.rem(x + step, 4) * 2 + core}

    def x_rows(c, step, first, size):
        return pl.ds(pl.multiple_of(core * 1024 + (c % 2) * 512 + lax.rem(x + step, 4) * 128 + first, 64), size)

    def send(src, dst, stage, sem, to):
        return pltpu.make_async_remote_copy(
            src_ref=src, dst_ref=dst, send_sem=rs_send.at[stage], recv_sem=sem, device_id=to
        )

    def step0(c):
        return send(dense.at[c // 2, part_rows(1 - core, c)], rs0.at[c], 0, rs0_sem.at[c], sibling)

    def step1(c, d):
        return send(dense.at[c // 2, x_rows(c, 2, 64 * d, 64)], rs1.at[c, d], 1, rs1_sem.at[c, d], at_x(1 + 2 * d))

    def step2(c, d):
        return send(dense.at[c // 2, x_rows(c, 1 + 2 * d, 0, 128)], rs2.at[c, d], 2, rs2_sem.at[c, d], at_x(1 + 2 * d))

    def begin(c):
        g = c // 2
        dense[g, part_rows(1 - core, c), :] = stack(g, part_rows(1 - core, c))
        step0(c).start()
        dense[g, part_rows(core, c), :] = stack(g, part_rows(core, c))

    def after0(c):
        g, rows = c // 2, part_rows(core, c)
        step0(c).wait_recv()
        dense[g, rows, :] = dense[g, rows, :] + rs0[c]
        for d in range(2):
            step1(c, d).start()

    def after1(c):
        g = c // 2
        for d in range(2):
            step1(c, d).wait_recv()
            rows = x_rows(c, 1 + 2 * d, 64 * d, 64)
            dense[g, rows, :] = dense[g, rows, :] + rs1[c, d]
            step2(c, d).start()

    def after2(c):
        g, mine = c // 2, x_rows(c, 0, 0, 128)
        for d in range(2):
            step2(c, d).wait_recv()
        dense[g, mine, :] = dense[g, mine, :] + (rs2[c, 0] + rs2[c, 1])
        own = pl.ds(pl.multiple_of(z * 16, 16), 16)
        first = core * 1024 + (c % 2) * 512 + x * 128
        rs3[c, own, :] = dense[g, pl.ds(pl.multiple_of(first + z * 16, 16), 16), :]
        for p in (4, 3, 5, 2, 6, 1, 7):
            there = lax.rem(z + p, 8)
            send(
                dense.at[g, pl.ds(pl.multiple_of(first + there * 16, 16), 16)], rs3.at[c, own],
                3, rs3_sem.at[c], {"trace": there * 8 + x * 2 + core},
            ).start()

    def after3(c):
        rows = pl.ds(0, 112)
        pltpu.make_async_copy(rs3.at[c, rows], rs3.at[c, rows], rs3_sem.at[c]).wait()
        total = rs3[c, 0:16, :]
        for s in range(1, 8):
            total = total + rs3[c, s * 16:(s + 1) * 16, :]
        stacked[c // 2, (c % 2) * 16:(c % 2 + 1) * 16, :] = 0.25 * total

    for step in range(12):
        for offset, stage in ((0, begin), (1, after0), (2, after1), (3, after2), (4, after3)):
            if 0 <= step - offset < 8:
                stage(step - offset)

    for part in range(2):
        out[48 + 32 * part:80 + 32 * part, :] = ordered(stacked[part], stacked[2 + part])
    for stage, ref in (
        (0, dense.at[:, pl.ds(0, 1024)]), (1, dense.at[:, pl.ds(0, 256)]),
        (2, dense.at[:, pl.ds(0, 512)]), (3, dense.at[:, pl.ds(0, 224)]),
    ):
        pending.append(pltpu.make_async_copy(ref, ref, rs_send.at[stage]).wait)
    for wait in pending:
        wait()


def shards(low_tab, high_tab, traces, shot_local, rec_slot, slot_station, cmp_owner, cmp_local):
    vmem = pltpu.VMEM
    dma = pltpu.SemaphoreType.DMA
    i32 = jnp.int32
    out = pl.pallas_call(
        kernel,
        out_shape=jax.ShapeDtypeStruct((112, 256), F32),
        in_specs=[pl.BlockSpec(memory_space=pl.ANY)] * 8,
        out_specs=pl.BlockSpec(memory_space=vmem),
        scratch_shapes=[
            vmem((TDEV, NT), F32), vmem((2, 128, 256), F32), vmem((2, 8, 256), F32), vmem((2, HALF, 512), BF16),
            vmem((TDEV, HALF), BF16), vmem((TDEV, HALF), BF16), vmem((TDEV, HALF), BF16), vmem((TDEV, HALF), BF16),
            vmem((TDEV, NB), F32), vmem((TDEV, 512), F32), vmem((2, TDEV, NB), F32), vmem((2, TDEV, NB), F32),
            vmem((1, TDEV), i32), vmem((1, TDEV), i32), vmem((1, SLOTS), i32), vmem((1, TDEV), i32), vmem((1, TDEV), i32),
            vmem((SLOTS, TDEV), BF16), vmem((TDEV, SLOTS), BF16), vmem((TDEV, 16), BF16),
            vmem((2048, TDEV), BF16), vmem((SLOTS, 32), BF16),
            vmem((64, 8, NB), F32), vmem((64, 8, NB), F32),
            vmem((3, SLOTS, NB), F32), vmem((3, SLOTS, NB), F32), vmem((4, SLOTS, NB), F32), vmem((4, SLOTS, NB), F32),
            vmem((1, TDEV), F32), vmem((4, 1, TDEV), F32),
            vmem((4, 2048, NB), F32), vmem((8, 512, NB), F32), vmem((8, 2, 64, NB), F32),
            vmem((8, 2, 128, NB), F32), vmem((8, 128, NB), F32), vmem((4, 32, NB), F32),
            dma((8,)), dma((2,)), dma((5,)), dma((8,)), dma((8,)), dma((3,)), dma((3,)),
            dma((4,)), dma((8,)), dma((8, 2)), dma((8, 2)), dma((8,)),
        ],
        compiler_params=pltpu.CompilerParams(
            collective_id=0, has_side_effects=True, vmem_limit_bytes=56 * 1024 * 1024
        ),
    )(
        traces, shot_local, rec_slot, slot_station, cmp_owner.reshape(1, TDEV), cmp_local.reshape(1, TDEV),
        low_tab, high_tab,
    )
    return out[0:16], out[16:48], jnp.stack([out[48:80], out[80:112]], axis=1)


def solution(mesh):
    low, high = twiddles()
    body = jax.shard_map(
        shards,
        mesh=mesh,
        in_specs=(
            P(), P(),
            P("trace", None),
            P("trace", None),
            P("trace", None),
            P("trace", None),
            P("trace", None),
            P("trace"),
        ),
        out_specs=(P("trace", "freq"), P("trace", "freq"), P("trace", None, "freq")),
        check_vma=False,
    )
    return functools.partial(body, low, high)
```

```python
import functools

import jax
import jax.numpy as jnp
import numpy as np
from jax import lax
from jax.experimental import pallas as pl
from jax.experimental.pallas import tpu as pltpu
from jax.sharding import PartitionSpec as P

NT = 2048
HALF = 1024
NB = 128
TDEV = 512
SLOTS = 256
F32 = jnp.float32
BF16 = jnp.bfloat16
NT_DIMS = (((1,), (1,)), ((), ()))
TN_DIMS = (((0,), (0,)), ((), ()))


def twiddles():
    bins = np.arange(4)[:, None, None] * 256 + np.arange(2)[None, :, None] + 2 * np.arange(NB)[None, None, :]
    low = -2.0 * np.pi * ((np.arange(128)[:, None] * bins[:, :, None, :]) % NT) / NT
    high = -2.0 * np.pi * ((128 * np.arange(8)[:, None] * bins[:, :, None, :]) % NT) / NT
    norm = NT**-0.5
    low = np.concatenate([np.cos(low), np.sin(low)], axis=-1) * norm
    high = np.concatenate([np.cos(high), np.sin(high)], axis=-1)
    return low.astype(np.float32), high.astype(np.float32)


def split(x, parts):
    out = []
    for i in range(parts):
        piece = x.astype(BF16)
        out.append(piece)
        if i + 1 < parts:
            x = x - piece.astype(F32)
    return out


def hot_dot(hot, x, parts=3, dims=(((1,), (0,)), ((), ()))):
    n = x.shape[1]
    full = lax.dot_general(hot, jnp.concatenate(split(x, parts), axis=1), dims, preferred_element_type=F32)
    total = full[:, :n]
    for i in range(1, parts):
        total = total + full[:, i * n:(i + 1) * n]
    return total


def iota(shape, axis):
    return lax.broadcasted_iota(jnp.int32, shape, axis)


def hot(condition):
    return jnp.where(condition, 1.0, 0.0).astype(BF16)


def kernel(
    traces, shot_in, slot_in, station_in, owner_in, local_in, low_tab, high_tab,
    shot_out, rec_out, cmp_out,
    xbuf, low, high, table, uhi, ulo, vhi, vlo, level, spec, logs, roots,
    shot_idx, slot_idx, station_idx, owner_idx, local_idx,
    slot_rows, slot_cols, shot_cols, cmp_hot, owner_cols,
    first_send, first_recv, sum_send, sum_recv, term_send, term_recv, q_send, q_recv,
    dense, rs0, rs1, rs2, rs3, rsz, zsum, rsx, stacked,
    x_sem, tab_sem, idx_sem, a2a_send, a2a_recv, q_ssem, q_rsem, rs0_sem, rs1_sem, rs2_sem, rs3_sem, rsz_sem, rsx_sem,
):
    me = lax.axis_index("trace")
    band = lax.axis_index("freq")
    z = lax.div(me, 8)
    x = lax.rem(lax.div(me, 2), 4)
    core = lax.rem(me, 2)
    pending = []

    def x_copy(c):
        rows = pl.ds(c * 64, 64)
        return pltpu.make_async_copy(traces.at[rows], xbuf.at[rows], x_sem.at[c])

    low_copy = pltpu.make_async_copy(low_tab.at[band], low, tab_sem.at[0])
    high_copy = pltpu.make_async_copy(high_tab.at[band], high, tab_sem.at[1])
    index_copies = [
        pltpu.make_async_copy(source, target, idx_sem.at[i])
        for i, (source, target) in enumerate((
            (shot_in, shot_idx), (slot_in, slot_idx), (station_in, station_idx), (owner_in, owner_idx), (local_in, local_idx),
        ))
    ]
    low_copy.start()
    high_copy.start()
    for c in range(8):
        x_copy(c).start()
    for copy in index_copies:
        copy.start()

    barrier = pltpu.get_barrier_semaphore()

    @pl.loop(1, 64)
    def _(p):
        pl.semaphore_signal(barrier, inc=1, device_id={"trace": lax.rem(me + p, 64)})

    for p in range(1, 4):
        pl.semaphore_signal(barrier, inc=1, device_id={"freq": lax.rem(band + p, 4)})

    def exchange(leg, source_of, target):
        sems = dict(send_sem=a2a_send.at[leg], recv_sem=a2a_recv.at[leg])

        def put(other):
            pltpu.make_async_remote_copy(
                src_ref=source_of(other), dst_ref=target(me), device_id={"trace": other}, **sems
            ).start()

        @pl.loop(0, 7)
        def _(k):
            side = 1 - 2 * lax.rem(k, 2)
            there = lax.rem(z + 12 + side * lax.div(k + 1, 2), 8) * 8
            for dx in (2, 1, 3, 0):
                for dc in (1, 0):
                    put(there + lax.rem(x + dx, 4) * 2 + lax.rem(core + dc, 2))

        for dx in (2, 1, 3, 0):
            for dc in (1, 0):
                if dx or dc:
                    put(z * 8 + lax.rem(x + dx, 4) * 2 + lax.rem(core + dc, 2))
        pltpu.make_async_copy(source_of(me), target(me), a2a_recv.at[leg]).start()

    def four(ref):
        return lambda d: ref.at[pl.ds(pl.multiple_of(d * 4, 4), 4)]

    def five(ref):
        return lambda d: ref.at[d, pl.ds(0, 5)]

    def exchange_rows(leg, source, target):
        exchange(leg, four(source), four(target))
        part = source.at[pl.ds(0, 252)]
        pending.append(pltpu.make_async_copy(part, part, a2a_send.at[leg]).wait)

    def arrived(leg, target):
        pltpu.make_async_copy(target, target, a2a_recv.at[leg]).wait()

    low_copy.wait()
    high_copy.wait()
    for h in range(2):
        low_re, low_im = low[h, :, :NB], low[h, :, NB:]
        for n1 in range(8):
            high_re, high_im = high[h, n1:n1 + 1, :NB], high[h, n1:n1 + 1, NB:]
            re_hi, re_lo = split(low_re * high_re - low_im * high_im, 2)
            im_hi, im_lo = split(low_re * high_im + low_im * high_re, 2)
            table[h, n1 * 128:(n1 + 1) * 128, :] = jnp.concatenate([re_hi, im_hi, re_lo, im_lo], axis=1)

    for copy in index_copies:
        copy.wait()
    shot_lane = shot_idx[...]
    slot_lane = slot_idx[...]
    station_lane = station_idx[...].astype(F32)
    slot_rows[...] = hot(iota((SLOTS, TDEV), 0) == slot_lane)
    shots = hot(iota((16, TDEV), 0) == shot_lane)
    slots = slot_rows[...]
    shot_count = jnp.sum(shots.astype(F32), axis=1, keepdims=True)
    counts = lax.dot_general(shots, slots, NT_DIMS, preferred_element_type=F32).astype(BF16)
    counts_t = lax.dot_general(slots, shots, NT_DIMS, preferred_element_type=F32).astype(BF16)
    slot_count = lax.dot_general(jnp.ones((8, TDEV), BF16), slots, NT_DIMS, preferred_element_type=F32)[0:1, :]
    meta = jnp.zeros((64, NB), F32)
    lane = iota((64, NB), 1)
    for c in range(4):
        named = iota((64, SLOTS), 1) == iota((64, SLOTS), 0) * 4 + c
        meta = jnp.where(lane == c, jnp.sum(jnp.where(named, station_lane, 0.0), axis=1, keepdims=True), meta)
        meta = jnp.where(lane == 4 + c, jnp.sum(jnp.where(named, slot_count, 0.0), axis=1, keepdims=True), meta)
    first_send[:, 4:5, :] = meta.reshape(64, 1, NB)

    sign = 1.0 - 2.0 * (iota((1, HALF), 1) & 1).astype(F32)

    @pl.loop(0, 8)
    def _(c):
        x_copy(c).wait()
        rows = pl.ds(pl.multiple_of(c * 64, 64), 64)
        first, second = xbuf[rows, :HALF], xbuf[rows, HALF:]
        u, v = first + second, first - second
        nyquist = jnp.sum(u * sign, axis=1, keepdims=True) * (1.0 / HALF)
        rest = u - nyquist * sign
        energy = jnp.sum(rest * rest + v * v, axis=1, keepdims=True) * 0.5
        mean = jnp.sum(u, axis=1, keepdims=True)
        level[rows, :] = jnp.broadcast_to((energy + mean * mean * (1.0 / NT)) * (0.01 * 0.5 / 1024.0), (64, NB))
        uhi[rows, :], ulo[rows, :] = split(u, 2)
        vhi[rows, :], vlo[rows, :] = split(v, 2)

    shot_sums, slot_sums, shot_terms = [None, None], [None, None], [None, None]
    for h, (hi, lo) in enumerate(((uhi, ulo), (vhi, vlo))):
        for part in range(2):
            rows = slice(part * 256, (part + 1) * 256)
            full = jnp.dot(hi[rows, :], table[h], preferred_element_type=F32)
            rest = jnp.dot(lo[rows, :], table[h, :, :256], preferred_element_type=F32)
            both = full[:, :256] + (full[:, 256:] + rest)
            spec[rows, h * 256:(h + 1) * 256] = both
            re, im = both[:, :NB], both[:, NB:]
            logs[h, rows, :] = jnp.log(re * re + im * im + level[rows, :])
        shot_sums[h] = hot_dot(shots, logs[h])
        slot_sums[h] = hot_dot(slot_rows[...], logs[h])
        shot_terms[h] = shot_sums[h] / shot_count
        sums = slot_sums[h] - hot_dot(counts_t, shot_terms[h])
        if h == 0:
            first_send[:, 0:4, :] = sums.reshape(64, 4, NB)
            pl.semaphore_wait(barrier, 66)
            exchange(0, five(first_send), five(first_recv))
            part = first_send.at[pl.ds(0, 63), pl.ds(0, 5)]
            pending.append(pltpu.make_async_copy(part, part, a2a_send.at[0]).wait)
        else:
            sum_send[0] = sums
            exchange_rows(1, sum_send.at[0], sum_recv.at[0])

    by_row = jnp.transpose(jnp.concatenate(
        [shot_lane.astype(F32), slot_lane.astype(F32), jnp.zeros((6, TDEV), F32)], axis=0
    ))
    shot_cols[...] = hot(iota((TDEV, 16), 1).astype(F32) == by_row[:, 0:1])
    slot_cols[...] = hot(iota((TDEV, SLOTS), 1).astype(F32) == by_row[:, 1:2])

    part = first_recv.at[:, pl.ds(0, 5)]
    pltpu.make_async_copy(part, part, a2a_recv.at[0]).wait()
    of_source = hot(lax.shift_right_logical(iota((SLOTS, 64), 0), 2) == iota((SLOTS, 64), 1))
    meta = hot_dot(of_source, first_recv[:, 4:5, :].reshape(64, NB), 2)
    lane, own = iota((SLOTS, NB), 1), iota((SLOTS, NB), 0) & 3
    station = jnp.sum(jnp.where(lane == own, meta, 0.0), axis=1, keepdims=True)
    count = jnp.sum(jnp.where(lane == own + 4, meta, 0.0), axis=1, keepdims=True)
    owner_cols[...] = hot(station == iota((SLOTS, 32), 1).astype(F32))
    owner = owner_cols[...]
    station_count = hot_dot(owner, jnp.broadcast_to(count, (SLOTS, NB)), 2, TN_DIMS)
    terms = [None, None]

    def at_owner(sweep, h):
        if sweep == 0 and h == 0:
            sums = first_recv[:, 0:4, :].reshape(SLOTS, NB)
        else:
            slot = sweep * 2 + h - 1
            arrived(1 if sweep == 0 else 4 + h, sum_recv.at[slot])
            sums = sum_recv[slot]
        terms[h] = hot_dot(owner, sums, 3, TN_DIMS) / station_count
        slot = sweep * 2 + h
        term_send[slot] = hot_dot(owner, terms[h])
        exchange_rows(2 + sweep * 4 + h, term_send.at[slot], term_recv.at[slot])

    def at_source(h):
        arrived(2 + h, term_recv.at[h])
        shot_terms[h] = (shot_sums[h] - hot_dot(counts, term_recv[h])) / shot_count
        sum_send[1 + h] = slot_sums[h] - hot_dot(counts_t, shot_terms[h])
        exchange_rows(4 + h, sum_send.at[1 + h], sum_recv.at[1 + h])

    at_owner(0, 0)
    at_owner(0, 1)
    for c in range(4):
        rows = slice(c * 512, (c + 1) * 512)
        owner_lane = owner_idx[...]
        local_lane = local_idx[...]
        place = (owner_lane & 1) * 1024 + lax.shift_right_logical(local_lane, 4) * 512 + (
            lax.shift_right_logical(owner_lane, 1) & 3) * 128 + lax.shift_right_logical(owner_lane, 3) * 16 + (local_lane & 15)
        cmp_hot[rows, :] = hot(iota((512, TDEV), 0) + c * 512 == place)
    at_source(0)
    at_source(1)
    at_owner(1, 0)
    at_owner(1, 1)

    k0, k1 = iota((256, 256), 0), iota((256, 256), 1)
    order = hot(k1 == 2 * (k0 & 127) + lax.shift_right_logical(k0, 7))

    def ordered(even, odd):
        total = jnp.zeros((even.shape[0], 256), F32)
        for piece in split(jnp.concatenate([even, odd], axis=1), 3):
            total = total + jnp.dot(piece, order, preferred_element_type=F32)
        return total

    shot_out[...] = ordered(shot_terms[0], shot_terms[1])
    rec_out[...] = ordered(terms[0], terms[1])
    shot_part = [hot_dot(shot_cols[...], shot_terms[h]) for h in range(2)]
    ones = jnp.ones((8, NB), BF16)
    partial = jnp.zeros((8, TDEV), F32)
    for h in range(2):
        arrived(6 + h, term_recv.at[2 + h])
        root = jnp.exp(0.5 * (shot_part[h] + hot_dot(slot_cols[...], term_recv[2 + h])))
        roots[h] = root
        for piece in split(root * root, 3):
            partial = partial + lax.dot_general(ones, piece, NT_DIMS, preferred_element_type=F32)
    q_send[...] = partial[0:1, :]
    q_recv[band] = partial[0:1, :]
    q_copies = []
    for p in (2, 1, 3):
        copy = pltpu.make_async_remote_copy(
            src_ref=q_send, dst_ref=q_recv.at[band], send_sem=q_ssem.at[p - 1], recv_sem=q_rsem.at[p - 1],
            device_id={"freq": lax.rem(band + p, 4)},
        )
        copy.start()
        q_copies.append(copy)
    for copy in q_copies:
        copy.wait()
    total = (q_recv[0] + q_recv[1]) + (q_recv[2] + q_recv[3])
    floor = jnp.transpose(jnp.broadcast_to(total, (8, TDEV)))[:, 0:1] * (0.3 / 1024.0)
    floor = jnp.broadcast_to(floor, (TDEV, NB))
    def deconvolve(h):
        root = roots[h]
        wiener = root / (root * root + floor)
        for c in range(2):
            cols = slice((2 * h + c) * NB, (2 * h + c + 1) * NB)
            spec[:, cols] = wiener * spec[:, cols]


    sibling = {"trace": me + 1 - 2 * core}

    def at_x(step):
        return {"trace": z * 8 + lax.rem(x + step, 4) * 2 + core}

    def at_z(step):
        return {"trace": lax.rem(z + step, 8) * 8 + x * 2 + core}

    def send(src, dst, sems, at, to):
        return pltpu.make_async_remote_copy(
            src_ref=src, dst_ref=dst, send_sem=sems.at[(0, *at)], recv_sem=sems.at[(1, *at)], device_id=to
        )

    pieces = ((0, 0, 2), (1, 1, 1), (2, 0, 2), (3, 0, 2), (1, 0, 1))

    def stack(i, of_core):
        g, first, size = pieces[i]
        rows = pl.ds(pl.multiple_of(of_core * 1024 + first * 512, 512), size * 512)
        parts = jnp.concatenate(split(spec[:, g * NB:(g + 1) * NB], 2), axis=1)
        full = jnp.dot(cmp_hot[rows, :], parts, preferred_element_type=F32)
        value = (full[:, :NB] + full[:, NB:]).reshape(size, 4, 8, 16, NB)
        dense[g, of_core, first:first + size] = value

    def step0(i):
        g, first, size = pieces[i]
        half = pl.ds(first, size)
        return send(dense.at[g, 1 - core, half], rs0.at[g, half], rs0_sem, (i,), sibling)

    def begin(i):
        stack(i, 1 - core)
        step0(i).start()
        stack(i, core)

    def join(i):
        g, first, size = pieces[i]
        step0(i).wait_recv()
        dense[g, core, first:first + size] = dense[g, core, first:first + size] + rs0[g, first:first + size]

    def far(g, size, step, d):
        if size == 2:
            return dense.at[g, core, d, lax.rem(x + step, 4)]
        return dense.at[g, core, 0, lax.rem(x + step, 4), pl.ds(4 * d, 4)]

    def step1(i, d):
        g, first, size = pieces[i]
        dst = rs1.at[g, d] if size == 2 else rs1.at[g, d, pl.ds(0, 4)]
        return send(far(g, size, 2, d), dst, rs1_sem, (i, d), at_x(1 + 2 * d))

    def step2(i, d):
        g, first, size = pieces[i]
        half = pl.ds(0, size)
        return send(
            dense.at[g, core, half, lax.rem(x + 1 + 2 * d, 4)], rs2.at[g, d, half], rs2_sem, (i, d), at_x(1 + 2 * d)
        )

    def after0(i):
        join(i)
        for d in range(2):
            step1(i, d).start()

    def after1(i):
        g, first, size = pieces[i]
        for d in range(2):
            step1(i, d).wait_recv()
            there = lax.rem(x + 1 + 2 * d, 4)
            if size == 2:
                dense[g, core, d, there] = dense[g, core, d, there] + rs1[g, d]
            else:
                rows = slice(4 * d, 4 * d + 4)
                dense[g, core, 0, there, rows] = dense[g, core, 0, there, rows] + rs1[g, d, 0:4]
            step2(i, d).start()

    def step3(i, p):
        g, first, size = pieces[i]
        half = pl.ds(0, size)
        return send(
            dense.at[g, core, half, x, lax.rem(z + p, 8)], rs3.at[g, z, half], rs3_sem, (i, p - 1), at_z(p)
        )

    def after2(i):
        g, first, size = pieces[i]
        for d in range(2):
            step2(i, d).wait_recv()
        dense[g, core, 0:size, x] = dense[g, core, 0:size, x] + (rs2[g, 0, 0:size] + rs2[g, 1, 0:size])
        for p in (4, 3, 5, 2, 6, 1, 7):
            step3(i, p).start()
        rs3[g, z, 0:size] = dense[g, core, 0:size, x, z]

    def after3(i):
        g, first, size = pieces[i]
        for p in range(1, 8):
            step3(i, p).wait_recv()
        total = rs3[g, 0, 0:size]
        for source in range(1, 8):
            total = total + rs3[g, source, 0:size]
        stacked[g, 0:16 * size, :] = 0.25 * total.reshape(16 * size, NB)

    def z_first(p):
        return send(dense.at[1, core, 1, :, lax.rem(z + p, 8)], rsz.at[z], rsz_sem, (p - 1,), at_z(p))

    def x_last(p):
        return send(zsum.at[lax.rem(x + p, 4)], rsx.at[x], rsx_sem, (p - 1,), at_x(p))

    def side0():
        join(1)
        for p in (4, 3, 5, 2, 6, 1, 7):
            z_first(p).start()
        rsz[z] = dense[1, core, 1, :, z]

    def side1():
        for p in range(1, 8):
            z_first(p).wait_recv()
        total = rsz[0]
        for source in range(1, 8):
            total = total + rsz[source]
        zsum[...] = total
        for p in (2, 1, 3):
            x_last(p).start()
        rsx[x] = zsum[x]

    def side2():
        for p in range(1, 4):
            x_last(p).wait_recv()
        stacked[1, 16:32, :] = 0.25 * ((rsx[0] + rsx[1]) + (rsx[2] + rsx[3]))

    deconvolve(0)
    begin(0)
    begin(1)
    after0(0)
    deconvolve(1)
    begin(2)
    side0()
    after0(2)
    after1(0)
    begin(3)
    after0(3)
    after1(2)
    begin(4)
    after0(4)
    after2(0)
    after1(3)
    side1()
    after1(4)
    after2(2)
    after3(0)
    after2(3)
    side2()
    after3(2)
    cmp_out[:, 0, :] = ordered(stacked[0], stacked[2])
    after2(4)
    after3(3)
    after3(4)
    cmp_out[:, 1, :] = ordered(stacked[1], stacked[3])

    for i in range(5):
        pending.append(step0(i).wait_send)
    for i in (0, 2, 3, 4):
        for d in range(2):
            pending.append(step1(i, d).wait_send)
            pending.append(step2(i, d).wait_send)
        for p in range(1, 8):
            pending.append(step3(i, p).wait_send)
    for p in range(1, 8):
        pending.append(z_first(p).wait_send)
    for p in range(1, 4):
        pending.append(x_last(p).wait_send)
    for wait in pending:
        wait()


def copy_kernel(a, b, c, x, y, z):
    x[...] = a[...]
    y[...] = b[...]
    z[...] = c[...]


def shards(low_tab, high_tab, traces, shot_local, rec_slot, slot_station, cmp_owner, cmp_local):
    vmem = pltpu.VMEM
    dma = pltpu.SemaphoreType.DMA
    i32 = jnp.int32
    outs = (
        jax.ShapeDtypeStruct((16, 256), F32),
        jax.ShapeDtypeStruct((32, 256), F32),
        jax.ShapeDtypeStruct((32, 2, 256), F32),
    )
    results = pl.pallas_call(
        kernel,
        out_shape=outs,
        in_specs=[pl.BlockSpec(memory_space=pl.ANY)] * 8,
        out_specs=(pl.BlockSpec(memory_space=vmem),) * 3,
        scratch_shapes=[
            vmem((TDEV, NT), F32), vmem((2, 128, 256), F32), vmem((2, 8, 256), F32), vmem((2, HALF, 512), BF16),
            vmem((TDEV, HALF), BF16), vmem((TDEV, HALF), BF16), vmem((TDEV, HALF), BF16), vmem((TDEV, HALF), BF16),
            vmem((TDEV, NB), F32), vmem((TDEV, 512), F32), vmem((2, TDEV, NB), F32), vmem((2, TDEV, NB), F32),
            vmem((1, TDEV), i32), vmem((1, TDEV), i32), vmem((1, SLOTS), i32), vmem((1, TDEV), i32), vmem((1, TDEV), i32),
            vmem((SLOTS, TDEV), BF16), vmem((TDEV, SLOTS), BF16), vmem((TDEV, 16), BF16),
            vmem((2048, TDEV), BF16), vmem((SLOTS, 32), BF16),
            vmem((64, 8, NB), F32), vmem((64, 8, NB), F32),
            vmem((3, SLOTS, NB), F32), vmem((3, SLOTS, NB), F32), vmem((4, SLOTS, NB), F32), vmem((4, SLOTS, NB), F32),
            vmem((1, TDEV), F32), vmem((4, 1, TDEV), F32),
            vmem((4, 2, 2, 4, 8, 16, NB), F32), vmem((4, 2, 4, 8, 16, NB), F32), vmem((4, 2, 8, 16, NB), F32),
            vmem((4, 2, 2, 8, 16, NB), F32), vmem((4, 8, 2, 16, NB), F32),
            vmem((8, 4, 16, NB), F32), vmem((4, 16, NB), F32), vmem((4, 16, NB), F32), vmem((4, 32, NB), F32),
            dma((8,)), dma((2,)), dma((5,)), dma((8,)), dma((8,)), dma((3,)), dma((3,)),
            dma((2, 5)), dma((2, 5, 2)), dma((2, 5, 2)), dma((2, 5, 7)), dma((2, 7)), dma((2, 3)),
        ],
        compiler_params=pltpu.CompilerParams(
            collective_id=0, has_side_effects=True, vmem_limit_bytes=56 * 1024 * 1024
        ),
    )(
        traces, shot_local, rec_slot, slot_station, cmp_owner.reshape(1, TDEV), cmp_local.reshape(1, TDEV),
        low_tab, high_tab,
    )
    return tuple(pl.pallas_call(
        copy_kernel,
        out_shape=outs,
        in_specs=[pl.BlockSpec(memory_space=vmem)] * 3,
        out_specs=(pl.BlockSpec(memory_space=vmem),) * 3,
    )(*results))


def solution(mesh):
    low, high = twiddles()
    body = jax.shard_map(
        shards,
        mesh=mesh,
        in_specs=(
            P(), P(),
            P("trace", None),
            P("trace", None),
            P("trace", None),
            P("trace", None),
            P("trace", None),
            P("trace"),
        ),
        out_specs=(P("trace", "freq"), P("trace", "freq"), P("trace", None, "freq")),
        check_vma=False,
    )
    return functools.partial(body, low, high)
```

```python
import functools

import jax
import jax.numpy as jnp
import numpy as np
from jax import lax
from jax.experimental import pallas as pl
from jax.experimental.pallas import tpu as pltpu
from jax.sharding import PartitionSpec as P

NT = 2048
HALF = 1024
NB = 128
TDEV = 512
SLOTS = 256
F32 = jnp.float32
BF16 = jnp.bfloat16
NT_DIMS = (((1,), (1,)), ((), ()))
TN_DIMS = (((0,), (0,)), ((), ()))


def twiddles():
    bins = np.arange(4)[:, None, None] * 256 + np.arange(2)[None, :, None] + 2 * np.arange(NB)[None, None, :]
    low = -2.0 * np.pi * ((np.arange(128)[:, None] * bins[:, :, None, :]) % NT) / NT
    high = -2.0 * np.pi * ((128 * np.arange(8)[:, None] * bins[:, :, None, :]) % NT) / NT
    norm = NT**-0.5
    low = np.concatenate([np.cos(low), np.sin(low)], axis=-1) * norm
    high = np.concatenate([np.cos(high), np.sin(high)], axis=-1)
    return low.astype(np.float32), high.astype(np.float32)


def split(x, parts):
    out = []
    for i in range(parts):
        piece = x.astype(BF16)
        out.append(piece)
        if i + 1 < parts:
            x = x - piece.astype(F32)
    return out


def hot_dot(hot, x, parts=3, dims=(((1,), (0,)), ((), ()))):
    n = x.shape[1]
    full = lax.dot_general(hot, jnp.concatenate(split(x, parts), axis=1), dims, preferred_element_type=F32)
    total = full[:, :n]
    for i in range(1, parts):
        total = total + full[:, i * n:(i + 1) * n]
    return total


def iota(shape, axis):
    return lax.broadcasted_iota(jnp.int32, shape, axis)


def hot(condition):
    return jnp.where(condition, 1.0, 0.0).astype(BF16)


def kernel(
    traces, shot_in, slot_in, station_in, owner_in, local_in, low_tab, high_tab,
    shot_out, rec_out, cmp_out,
    xbuf, low, high, table, uhi, ulo, vhi, vlo, level, spec, logs, roots,
    shot_idx, slot_idx, station_idx, owner_idx, local_idx,
    slot_rows, slot_cols, shot_cols, cmp_hot, owner_cols,
    first_send, first_recv, sum_send, sum_recv, term_send, term_recv, q_send, q_recv,
    dense, rs0, rs1, rs2, rs3, rsz, zsum, rsx, stacked, shot_buf, rec_buf, cmp_buf,
    x_sem, tab_sem, idx_sem, a2a_send, a2a_recv, q_ssem, q_rsem, rs0_sem, rs1_sem, rs2_sem, rs3_sem, rsz_sem, rsx_sem, out_sem,
):
    me = lax.axis_index("trace")
    band = lax.axis_index("freq")
    z = lax.div(me, 8)
    x = lax.rem(lax.div(me, 2), 4)
    core = lax.rem(me, 2)
    pending = []

    def x_copy(c):
        rows = pl.ds(c * 64, 64)
        return pltpu.make_async_copy(traces.at[rows], xbuf.at[rows], x_sem.at[c])

    low_copy = pltpu.make_async_copy(low_tab.at[band], low, tab_sem.at[0])
    high_copy = pltpu.make_async_copy(high_tab.at[band], high, tab_sem.at[1])
    index_copies = [
        pltpu.make_async_copy(source, target, idx_sem.at[i])
        for i, (source, target) in enumerate((
            (shot_in, shot_idx), (slot_in, slot_idx), (station_in, station_idx), (owner_in, owner_idx), (local_in, local_idx),
        ))
    ]
    low_copy.start()
    high_copy.start()
    for c in range(8):
        x_copy(c).start()
    for copy in index_copies:
        copy.start()

    barrier = pltpu.get_barrier_semaphore()

    @pl.loop(1, 64)
    def _(p):
        pl.semaphore_signal(barrier, inc=1, device_id={"trace": lax.rem(me + p, 64)})

    for p in range(1, 4):
        pl.semaphore_signal(barrier, inc=1, device_id={"freq": lax.rem(band + p, 4)})

    def exchange(leg, source_of, target, beside=None):
        sems = dict(send_sem=a2a_send.at[leg], recv_sem=a2a_recv.at[leg])

        def put(other):
            pltpu.make_async_remote_copy(
                src_ref=source_of(other), dst_ref=target(me), device_id={"trace": other}, **sems
            ).start()

        @pl.loop(0, 7)
        def _(k):
            side = 1 - 2 * lax.rem(k, 2)
            there = lax.rem(z + 12 + side * lax.div(k + 1, 2), 8) * 8
            for dx in (2, 1, 3, 0):
                for dc in (1, 0):
                    put(there + lax.rem(x + dx, 4) * 2 + lax.rem(core + dc, 2))
            if beside is not None:
                beside(k)

        for dx in (2, 1, 3, 0):
            for dc in (1, 0):
                if dx or dc:
                    put(z * 8 + lax.rem(x + dx, 4) * 2 + lax.rem(core + dc, 2))
        pltpu.make_async_copy(source_of(me), target(me), a2a_recv.at[leg]).start()
        if beside is not None:
            beside(7)

    def four(ref):
        return lambda d: ref.at[pl.ds(pl.multiple_of(d * 4, 4), 4)]

    def five(ref):
        return lambda d: ref.at[d, pl.ds(0, 5)]

    def exchange_rows(leg, source, target):
        exchange(leg, four(source), four(target))
        part = source.at[pl.ds(0, 252)]
        pending.append(pltpu.make_async_copy(part, part, a2a_send.at[leg]).wait)

    def arrived(leg, target):
        pltpu.make_async_copy(target, target, a2a_recv.at[leg]).wait()

    low_copy.wait()
    high_copy.wait()
    for h in range(2):
        low_re, low_im = low[h, :, :NB], low[h, :, NB:]
        for n1 in range(8):
            high_re, high_im = high[h, n1:n1 + 1, :NB], high[h, n1:n1 + 1, NB:]
            re_hi, re_lo = split(low_re * high_re - low_im * high_im, 2)
            im_hi, im_lo = split(low_re * high_im + low_im * high_re, 2)
            table[h, n1 * 128:(n1 + 1) * 128, :] = jnp.concatenate([re_hi, im_hi, re_lo, im_lo], axis=1)

    for copy in index_copies:
        copy.wait()
    shot_lane = shot_idx[...]
    slot_lane = slot_idx[...]
    station_lane = station_idx[...].astype(F32)
    slot_rows[...] = hot(iota((SLOTS, TDEV), 0) == slot_lane)
    shots = hot(iota((16, TDEV), 0) == shot_lane)
    slots = slot_rows[...]
    shot_count = jnp.sum(shots.astype(F32), axis=1, keepdims=True)
    counts = lax.dot_general(shots, slots, NT_DIMS, preferred_element_type=F32).astype(BF16)
    counts_t = lax.dot_general(slots, shots, NT_DIMS, preferred_element_type=F32).astype(BF16)
    slot_count = lax.dot_general(jnp.ones((8, TDEV), BF16), slots, NT_DIMS, preferred_element_type=F32)[0:1, :]
    meta = jnp.zeros((64, NB), F32)
    lane = iota((64, NB), 1)
    for c in range(4):
        named = iota((64, SLOTS), 1) == iota((64, SLOTS), 0) * 4 + c
        meta = jnp.where(lane == c, jnp.sum(jnp.where(named, station_lane, 0.0), axis=1, keepdims=True), meta)
        meta = jnp.where(lane == 4 + c, jnp.sum(jnp.where(named, slot_count, 0.0), axis=1, keepdims=True), meta)
    first_send[:, 4:5, :] = meta.reshape(64, 1, NB)

    sign = 1.0 - 2.0 * (iota((1, HALF), 1) & 1).astype(F32)

    @pl.loop(0, 8)
    def _(c):
        x_copy(c).wait()
        rows = pl.ds(pl.multiple_of(c * 64, 64), 64)
        first, second = xbuf[rows, :HALF], xbuf[rows, HALF:]
        u, v = first + second, first - second
        nyquist = jnp.sum(u * sign, axis=1, keepdims=True) * (1.0 / HALF)
        rest = u - nyquist * sign
        energy = jnp.sum(rest * rest + v * v, axis=1, keepdims=True) * 0.5
        mean = jnp.sum(u, axis=1, keepdims=True)
        level[rows, :] = jnp.broadcast_to((energy + mean * mean * (1.0 / NT)) * (0.01 * 0.5 / 1024.0), (64, NB))
        uhi[rows, :], ulo[rows, :] = split(u, 2)
        vhi[rows, :], vlo[rows, :] = split(v, 2)

    shot_sums, slot_sums, shot_terms = [None, None], [None, None], [None, None]
    def transform(h, hi, lo, rows):
        full = jnp.dot(hi[rows, :], table[h], preferred_element_type=F32)
        rest = jnp.dot(lo[rows, :], table[h, :, :256], preferred_element_type=F32)
        both = full[:, :256] + (full[:, 256:] + rest)
        spec[rows, h * 256:(h + 1) * 256] = both
        re, im = both[:, :NB], both[:, NB:]
        logs[h, rows, :] = jnp.log(re * re + im * im + level[rows, :])

    def odd_rows(k):
        transform(1, vhi, vlo, pl.ds(k * 64 if isinstance(k, int) else pl.multiple_of(k * 64, 64), 64))

    for part in range(2):
        transform(0, uhi, ulo, pl.ds(part * 256, 256))
    for h in range(2):
        shot_sums[h] = hot_dot(shots, logs[h])
        slot_sums[h] = hot_dot(slot_rows[...], logs[h])
        shot_terms[h] = shot_sums[h] / shot_count
        sums = slot_sums[h] - hot_dot(counts_t, shot_terms[h])
        if h == 0:
            first_send[:, 0:4, :] = sums.reshape(64, 4, NB)
            pl.semaphore_wait(barrier, 66)
            exchange(0, five(first_send), five(first_recv), odd_rows)
            part = first_send.at[pl.ds(0, 63), pl.ds(0, 5)]
            pending.append(pltpu.make_async_copy(part, part, a2a_send.at[0]).wait)
        else:
            sum_send[0] = sums
            exchange_rows(1, sum_send.at[0], sum_recv.at[0])

    by_row = jnp.transpose(jnp.concatenate(
        [shot_lane.astype(F32), slot_lane.astype(F32), jnp.zeros((6, TDEV), F32)], axis=0
    ))
    shot_cols[...] = hot(iota((TDEV, 16), 1).astype(F32) == by_row[:, 0:1])
    slot_cols[...] = hot(iota((TDEV, SLOTS), 1).astype(F32) == by_row[:, 1:2])

    part = first_recv.at[:, pl.ds(0, 5)]
    pltpu.make_async_copy(part, part, a2a_recv.at[0]).wait()
    of_source = hot(lax.shift_right_logical(iota((SLOTS, 64), 0), 2) == iota((SLOTS, 64), 1))
    meta = hot_dot(of_source, first_recv[:, 4:5, :].reshape(64, NB), 2)
    lane, own = iota((SLOTS, NB), 1), iota((SLOTS, NB), 0) & 3
    station = jnp.sum(jnp.where(lane == own, meta, 0.0), axis=1, keepdims=True)
    count = jnp.sum(jnp.where(lane == own + 4, meta, 0.0), axis=1, keepdims=True)
    owner_cols[...] = hot(station == iota((SLOTS, 32), 1).astype(F32))
    owner = owner_cols[...]
    station_count = hot_dot(owner, jnp.broadcast_to(count, (SLOTS, NB)), 2, TN_DIMS)
    terms = [None, None]

    def at_owner(sweep, h):
        if sweep == 0 and h == 0:
            sums = first_recv[:, 0:4, :].reshape(SLOTS, NB)
        else:
            slot = sweep * 2 + h - 1
            arrived(1 if sweep == 0 else 4 + h, sum_recv.at[slot])
            sums = sum_recv[slot]
        terms[h] = hot_dot(owner, sums, 3, TN_DIMS) / station_count
        slot = sweep * 2 + h
        term_send[slot] = hot_dot(owner, terms[h])
        exchange_rows(2 + sweep * 4 + h, term_send.at[slot], term_recv.at[slot])

    def at_source(h):
        arrived(2 + h, term_recv.at[h])
        shot_terms[h] = (shot_sums[h] - hot_dot(counts, term_recv[h])) / shot_count
        sum_send[1 + h] = slot_sums[h] - hot_dot(counts_t, shot_terms[h])
        exchange_rows(4 + h, sum_send.at[1 + h], sum_recv.at[1 + h])

    at_owner(0, 0)
    at_owner(0, 1)
    for c in range(4):
        rows = slice(c * 512, (c + 1) * 512)
        owner_lane = owner_idx[...]
        local_lane = local_idx[...]
        place = (owner_lane & 1) * 1024 + lax.shift_right_logical(local_lane, 4) * 512 + (
            lax.shift_right_logical(owner_lane, 1) & 3) * 128 + lax.shift_right_logical(owner_lane, 3) * 16 + (local_lane & 15)
        cmp_hot[rows, :] = hot(iota((512, TDEV), 0) + c * 512 == place)
    at_source(0)
    at_source(1)
    at_owner(1, 0)
    at_owner(1, 1)

    k0, k1 = iota((256, 256), 0), iota((256, 256), 1)
    order = hot(k1 == 2 * (k0 & 127) + lax.shift_right_logical(k0, 7))

    def ordered(even, odd):
        total = jnp.zeros((even.shape[0], 256), F32)
        for piece in split(jnp.concatenate([even, odd], axis=1), 3):
            total = total + jnp.dot(piece, order, preferred_element_type=F32)
        return total

    shot_buf[...] = ordered(shot_terms[0], shot_terms[1])
    rec_buf[...] = ordered(terms[0], terms[1])
    out_copies = [
        pltpu.make_async_copy(source, target, out_sem.at[i])
        for i, (source, target) in enumerate(((shot_buf, shot_out), (rec_buf, rec_out), (cmp_buf, cmp_out)))
    ]
    out_copies[0].start()
    out_copies[1].start()
    shot_part = [hot_dot(shot_cols[...], shot_terms[h]) for h in range(2)]
    ones = jnp.ones((8, NB), BF16)
    partial = jnp.zeros((8, TDEV), F32)
    for h in range(2):
        arrived(6 + h, term_recv.at[2 + h])
        root = jnp.exp(0.5 * (shot_part[h] + hot_dot(slot_cols[...], term_recv[2 + h])))
        roots[h] = root
        for piece in split(root * root, 3):
            partial = partial + lax.dot_general(ones, piece, NT_DIMS, preferred_element_type=F32)
    q_send[...] = partial[0:1, :]
    q_recv[band] = partial[0:1, :]
    q_copies = []
    for p in (2, 1, 3):
        copy = pltpu.make_async_remote_copy(
            src_ref=q_send, dst_ref=q_recv.at[band], send_sem=q_ssem.at[p - 1], recv_sem=q_rsem.at[p - 1],
            device_id={"freq": lax.rem(band + p, 4)},
        )
        copy.start()
        q_copies.append(copy)
    for copy in q_copies:
        copy.wait()
    total = (q_recv[0] + q_recv[1]) + (q_recv[2] + q_recv[3])
    floor = jnp.transpose(jnp.broadcast_to(total, (8, TDEV)))[:, 0:1] * (0.3 / 1024.0)
    floor = jnp.broadcast_to(floor, (TDEV, NB))
    def deconvolve(h):
        root = roots[h]
        wiener = root / (root * root + floor)
        for c in range(2):
            cols = slice((2 * h + c) * NB, (2 * h + c + 1) * NB)
            spec[:, cols] = wiener * spec[:, cols]


    sibling = {"trace": me + 1 - 2 * core}

    def at_x(step):
        return {"trace": z * 8 + lax.rem(x + step, 4) * 2 + core}

    def at_z(step):
        return {"trace": lax.rem(z + step, 8) * 8 + x * 2 + core}

    def send(src, dst, sems, at, to):
        return pltpu.make_async_remote_copy(
            src_ref=src, dst_ref=dst, send_sem=sems.at[(0, *at)], recv_sem=sems.at[(1, *at)], device_id=to
        )

    pieces = ((0, 0, 1), (1, 0, 2), (0, 1, 1), (2, 0, 2), (3, 0, 1), (3, 1, 1))

    def stack(i, of_core):
        g, first, size = pieces[i]
        rows = pl.ds(pl.multiple_of(of_core * 1024 + first * 512, 512), size * 512)
        parts = jnp.concatenate(split(spec[:, g * NB:(g + 1) * NB], 2), axis=1)
        full = jnp.dot(cmp_hot[rows, :], parts, preferred_element_type=F32)
        value = (full[:, :NB] + full[:, NB:]).reshape(size, 4, 8, 16, NB)
        dense[g, of_core, first:first + size] = value

    def step0(i):
        g, first, size = pieces[i]
        half = pl.ds(first, size)
        return send(dense.at[g, 1 - core, half], rs0.at[g, half], rs0_sem, (i,), sibling)

    def begin(i):
        stack(i, 1 - core)
        step0(i).start()
        stack(i, core)

    def join(i):
        g, first, size = pieces[i]
        step0(i).wait_recv()
        dense[g, core, first:first + size] = dense[g, core, first:first + size] + rs0[g, first:first + size]

    def far(g, first, size, step, d):
        if size == 2:
            return dense.at[g, core, d, lax.rem(x + step, 4)]
        return dense.at[g, core, first, lax.rem(x + step, 4), pl.ds(4 * d, 4)]

    def step1(i, d):
        g, first, size = pieces[i]
        dst = rs1.at[g, d] if size == 2 else rs1.at[g, d, pl.ds(4 * first, 4)]
        return send(far(g, first, size, 2, d), dst, rs1_sem, (i, d), at_x(1 + 2 * d))

    def step2(i, d):
        g, first, size = pieces[i]
        half = pl.ds(first, size)
        return send(
            dense.at[g, core, half, lax.rem(x + 1 + 2 * d, 4)], rs2.at[g, d, half], rs2_sem, (i, d), at_x(1 + 2 * d)
        )

    def after0(i):
        join(i)
        for d in range(2):
            step1(i, d).start()

    def after1(i):
        g, first, size = pieces[i]
        for d in range(2):
            step1(i, d).wait_recv()
            there = lax.rem(x + 1 + 2 * d, 4)
            if size == 2:
                dense[g, core, d, there] = dense[g, core, d, there] + rs1[g, d]
            else:
                rows = slice(4 * d, 4 * d + 4)
                dense[g, core, first, there, rows] = dense[g, core, first, there, rows] + rs1[g, d, 4 * first:4 * first + 4]
            step2(i, d).start()

    def step3(i, p):
        g, first, size = pieces[i]
        half = pl.ds(first, size)
        return send(
            dense.at[g, core, half, x, lax.rem(z + p, 8)], rs3.at[g, z, half], rs3_sem, (i,), at_z(p)
        )

    def after2(i):
        g, first, size = pieces[i]
        for d in range(2):
            step2(i, d).wait_recv()
        last = first + size
        dense[g, core, first:last, x] = dense[g, core, first:last, x] + (rs2[g, 0, first:last] + rs2[g, 1, first:last])
        for p in (4, 3, 5, 2, 6, 1, 7):
            step3(i, p).start()
        rs3[g, z, first:last] = dense[g, core, first:last, x, z]

    def step3_bytes(i, way):
        g, first, size = pieces[i]
        part = rs3.at[g, pl.ds(0, 7), pl.ds(first, size)]
        return pltpu.make_async_copy(part, part, rs3_sem.at[way, i])

    def after3(i):
        g, first, size = pieces[i]
        last = first + size
        step3_bytes(i, 1).wait()
        total = rs3[g, 0, first:last]
        for source in range(1, 8):
            total = total + rs3[g, source, first:last]
        stacked[g, 16 * first:16 * last, :] = 0.25 * total.reshape(16 * size, NB)

    def round_z(flow, step):
        there = lax.rem(z + 4 - step, 8) if flow == 0 else lax.rem(z + 5 + step, 8)
        return send(
            dense.at[1, core, :, :, there], rsz.at[flow, step], rsz_sem, (flow, step), at_z(1 if flow == 0 else 7)
        )

    def x_last(p):
        return send(zsum.at[:, lax.rem(x + p, 4)], rsx.at[x], rsx_sem, (p - 1,), at_x(p))

    def side0():
        join(1)
        round_z(0, 0).start()
        round_z(1, 0).start()

    def side(step):
        for flow in range(2):
            if step <= 3:
                round_z(flow, step - 1).wait_recv()
                there = lax.rem(z + 4 - step, 8) if flow == 0 else lax.rem(z + 5 + step, 8)
                dense[1, core, :, :, there] = dense[1, core, :, :, there] + rsz[flow, step - 1]
                if flow == 0 or step < 3:
                    round_z(flow, step).start()

    def side4():
        round_z(0, 3).wait_recv()
        zsum[...] = dense[1, core, :, :, z] + rsz[0, 3]
        for p in (2, 1, 3):
            x_last(p).start()
        rsx[x] = zsum[:, x]

    def side5():
        for p in range(1, 4):
            x_last(p).wait_recv()
        stacked[1] = 0.25 * ((rsx[0] + rsx[1]) + (rsx[2] + rsx[3])).reshape(32, NB)

    deconvolve(0)
    begin(0)
    begin(1)
    after0(0)
    begin(2)
    side0()
    deconvolve(1)
    after0(2)
    begin(3)
    after1(0)
    begin(4)
    after0(3)
    after1(2)
    side(1)
    begin(5)
    after0(4)
    after2(0)
    after1(3)
    after0(5)
    after2(2)
    side(2)
    after1(4)
    after3(0)
    after1(5)
    side(3)
    after2(3)
    after3(2)
    side4()
    after2(4)
    after3(3)
    cmp_buf[:, 0, :] = ordered(stacked[0], stacked[2])
    after2(5)
    for i in range(6):
        pending.append(step0(i).wait_send)
    for i in (0, 2, 3, 4, 5):
        for d in range(2):
            pending.append(step1(i, d).wait_send)
            pending.append(step2(i, d).wait_send)
        if i < 5:
            pending.append(step3_bytes(i, 0).wait)
    for step in range(4):
        pending.append(round_z(0, step).wait_send)
    for step in range(3):
        pending.append(round_z(1, step).wait_send)
    for p in range(1, 4):
        pending.append(x_last(p).wait_send)
    for wait in pending:
        wait()
    side5()
    after3(4)
    after3(5)
    cmp_buf[:, 1, :] = ordered(stacked[1], stacked[3])
    out_copies[2].start()
    step3_bytes(5, 0).wait()
    for copy in out_copies:
        copy.wait()


def copy_kernel(a, b, c, x, y, z, p, q, r, sems):
    triples = ((a, p, x), (b, q, y), (c, r, z))
    reads = [pltpu.make_async_copy(s, m, sems.at[0, i]) for i, (s, m, t) in enumerate(triples)]
    writes = [pltpu.make_async_copy(m, t, sems.at[1, i]) for i, (s, m, t) in enumerate(triples)]
    for copy in reads:
        copy.start()
    for read, write in zip(reads, writes):
        read.wait()
        write.start()
    for copy in writes:
        copy.wait()


def shards(low_tab, high_tab, traces, shot_local, rec_slot, slot_station, cmp_owner, cmp_local):
    vmem = pltpu.VMEM
    dma = pltpu.SemaphoreType.DMA
    i32 = jnp.int32
    outs = (
        jax.ShapeDtypeStruct((16, 256), F32),
        jax.ShapeDtypeStruct((32, 256), F32),
        jax.ShapeDtypeStruct((32, 2, 256), F32),
    )
    results = pl.pallas_call(
        kernel,
        out_shape=outs,
        in_specs=[pl.BlockSpec(memory_space=pl.ANY)] * 8,
        out_specs=(pl.BlockSpec(memory_space=pl.ANY),) * 3,
        scratch_shapes=[
            vmem((TDEV, NT), F32), vmem((2, 128, 256), F32), vmem((2, 8, 256), F32), vmem((2, HALF, 512), BF16),
            vmem((TDEV, HALF), BF16), vmem((TDEV, HALF), BF16), vmem((TDEV, HALF), BF16), vmem((TDEV, HALF), BF16),
            vmem((TDEV, NB), F32), vmem((TDEV, 512), F32), vmem((2, TDEV, NB), F32), vmem((2, TDEV, NB), F32),
            vmem((1, TDEV), i32), vmem((1, TDEV), i32), vmem((1, SLOTS), i32), vmem((1, TDEV), i32), vmem((1, TDEV), i32),
            vmem((SLOTS, TDEV), BF16), vmem((TDEV, SLOTS), BF16), vmem((TDEV, 16), BF16),
            vmem((2048, TDEV), BF16), vmem((SLOTS, 32), BF16),
            vmem((64, 8, NB), F32), vmem((64, 8, NB), F32),
            vmem((3, SLOTS, NB), F32), vmem((3, SLOTS, NB), F32), vmem((4, SLOTS, NB), F32), vmem((4, SLOTS, NB), F32),
            vmem((1, TDEV), F32), vmem((4, 1, TDEV), F32),
            vmem((4, 2, 2, 4, 8, 16, NB), F32), vmem((4, 2, 4, 8, 16, NB), F32), vmem((4, 2, 8, 16, NB), F32),
            vmem((4, 2, 2, 8, 16, NB), F32), vmem((4, 8, 2, 16, NB), F32),
            vmem((2, 4, 2, 4, 16, NB), F32), vmem((2, 4, 16, NB), F32), vmem((4, 2, 16, NB), F32), vmem((4, 32, NB), F32),
            vmem((16, 256), F32), vmem((32, 256), F32), vmem((32, 2, 256), F32),
            dma((8,)), dma((2,)), dma((5,)), dma((8,)), dma((8,)), dma((3,)), dma((3,)),
            dma((2, 6)), dma((2, 6, 2)), dma((2, 6, 2)), dma((2, 6)), dma((2, 2, 4)), dma((2, 3)), dma((3,)),
        ],
        compiler_params=pltpu.CompilerParams(
            collective_id=0, has_side_effects=True, vmem_limit_bytes=56 * 1024 * 1024
        ),
    )(
        traces, shot_local, rec_slot, slot_station, cmp_owner.reshape(1, TDEV), cmp_local.reshape(1, TDEV),
        low_tab, high_tab,
    )
    return tuple(pl.pallas_call(
        copy_kernel,
        out_shape=outs,
        in_specs=[pl.BlockSpec(memory_space=pl.ANY)] * 3,
        out_specs=(pl.BlockSpec(memory_space=pl.ANY),) * 3,
        scratch_shapes=[vmem((16, 256), F32), vmem((32, 256), F32), vmem((32, 2, 256), F32), dma((2, 3))],
        compiler_params=pltpu.CompilerParams(vmem_limit_bytes=56 * 1024 * 1024),
    )(*results))


def solution(mesh):
    low, high = twiddles()
    body = jax.shard_map(
        shards,
        mesh=mesh,
        in_specs=(
            P(), P(),
            P("trace", None),
            P("trace", None),
            P("trace", None),
            P("trace", None),
            P("trace", None),
            P("trace"),
        ),
        out_specs=(P("trace", "freq"), P("trace", "freq"), P("trace", None, "freq")),
        check_vma=False,
    )
    return functools.partial(body, low, high)
```

```python
import functools

import jax
import jax.numpy as jnp
import numpy as np
from jax import lax
from jax.experimental import pallas as pl
from jax.experimental.pallas import tpu as pltpu
from jax.sharding import PartitionSpec as P

NT = 2048
HALF = 1024
NB = 128
TDEV = 512
SLOTS = 256
F32 = jnp.float32
BF16 = jnp.bfloat16
NT_DIMS = (((1,), (1,)), ((), ()))
TN_DIMS = (((0,), (0,)), ((), ()))


def twiddles():
    bins = np.arange(4)[:, None, None] * 256 + np.arange(2)[None, :, None] + 2 * np.arange(NB)[None, None, :]
    low = -2.0 * np.pi * ((np.arange(128)[:, None] * bins[:, :, None, :]) % NT) / NT
    high = -2.0 * np.pi * ((128 * np.arange(8)[:, None] * bins[:, :, None, :]) % NT) / NT
    norm = NT**-0.5
    low = np.concatenate([np.cos(low), np.sin(low)], axis=-1) * norm
    high = np.concatenate([np.cos(high), np.sin(high)], axis=-1)
    return low.astype(np.float32), high.astype(np.float32)


def split(x, parts):
    out = []
    for i in range(parts):
        piece = x.astype(BF16)
        out.append(piece)
        if i + 1 < parts:
            x = x - piece.astype(F32)
    return out


def hot_dot(hot, x, parts=3, dims=(((1,), (0,)), ((), ()))):
    n = x.shape[1]
    full = lax.dot_general(hot, jnp.concatenate(split(x, parts), axis=1), dims, preferred_element_type=F32)
    total = full[:, :n]
    for i in range(1, parts):
        total = total + full[:, i * n:(i + 1) * n]
    return total


def iota(shape, axis):
    return lax.broadcasted_iota(jnp.int32, shape, axis)


def hot(condition):
    return jnp.where(condition, 1.0, 0.0).astype(BF16)


def kernel(
    traces, shot_in, slot_in, station_in, owner_in, local_in, low_tab, high_tab,
    shot_out, rec_out, cmp_out,
    xbuf, low, high, table, uhi, ulo, vhi, vlo, level, spec, logs, roots,
    shot_idx, slot_idx, station_idx, owner_idx, local_idx,
    slot_rows, slot_cols, shot_cols, cmp_hot, owner_cols,
    first_send, first_recv, sum_send, sum_recv, term_send, term_recv, q_send, q_recv,
    dense, rs0, rs1, rs2, rs3, rsz, zsum, rsx, stacked, shot_buf, rec_buf, cmp_buf,
    x_sem, tab_sem, idx_sem, a2a_send, a2a_recv, q_ssem, q_rsem, rs0_sem, rs1_sem, rs2_sem, rs3_sem, rsz_sem, rsx_sem, out_sem,
):
    me = lax.axis_index("trace")
    band = lax.axis_index("freq")
    z = lax.div(me, 8)
    x = lax.rem(lax.div(me, 2), 4)
    core = lax.rem(me, 2)
    pending = []
    places = [lax.rem(x + dx, 4) * 2 + lax.rem(core + dc, 2) for dx in (2, 1, 3, 0) for dc in (1, 0)]

    def x_copy(c):
        rows = pl.ds(c * 64, 64)
        return pltpu.make_async_copy(traces.at[rows], xbuf.at[rows], x_sem.at[c])

    low_copy = pltpu.make_async_copy(low_tab.at[band], low, tab_sem.at[0])
    high_copy = pltpu.make_async_copy(high_tab.at[band], high, tab_sem.at[1])
    index_copies = [
        pltpu.make_async_copy(source, target, idx_sem.at[i])
        for i, (source, target) in enumerate((
            (shot_in, shot_idx), (slot_in, slot_idx), (station_in, station_idx), (owner_in, owner_idx), (local_in, local_idx),
        ))
    ]
    low_copy.start()
    high_copy.start()
    for c in range(8):
        x_copy(c).start()
    for copy in index_copies:
        copy.start()

    barrier = pltpu.get_barrier_semaphore()

    @pl.loop(1, 64)
    def _(p):
        pl.semaphore_signal(barrier, inc=1, device_id={"trace": lax.rem(me + p, 64)})

    for p in range(1, 4):
        pl.semaphore_signal(barrier, inc=1, device_id={"freq": lax.rem(band + p, 4)})

    def exchange(leg, source_of, target, beside=None):
        sems = dict(send_sem=a2a_send.at[leg], recv_sem=a2a_recv.at[leg])

        def put(other):
            pltpu.make_async_remote_copy(
                src_ref=source_of(other), dst_ref=target(me), device_id={"trace": other}, **sems
            ).start()

        @pl.loop(0, 7)
        def _(k):
            side = 1 - 2 * lax.rem(k, 2)
            there = lax.rem(z + 12 + side * lax.div(k + 1, 2), 8) * 8
            for place in places:
                put(there + place)
            if beside is not None:
                beside(k)

        for place in places[:7]:
            put(z * 8 + place)
        pltpu.make_async_copy(source_of(me), target(me), a2a_recv.at[leg]).start()
        if beside is not None:
            beside(7)

    def four(ref):
        return lambda d: ref.at[pl.ds(pl.multiple_of(d * 4, 4), 4)]

    def five(ref):
        return lambda d: ref.at[d, pl.ds(0, 5)]

    def exchange_rows(leg, source, target):
        exchange(leg, four(source), four(target))
        part = source.at[pl.ds(0, 252)]
        pending.append(pltpu.make_async_copy(part, part, a2a_send.at[leg]).wait)

    def arrived(leg, target):
        pltpu.make_async_copy(target, target, a2a_recv.at[leg]).wait()

    low_copy.wait()
    high_copy.wait()
    for h in range(2):
        low_re, low_im = low[h, :, :NB], low[h, :, NB:]
        for n1 in range(8):
            high_re, high_im = high[h, n1:n1 + 1, :NB], high[h, n1:n1 + 1, NB:]
            re_hi, re_lo = split(low_re * high_re - low_im * high_im, 2)
            im_hi, im_lo = split(low_re * high_im + low_im * high_re, 2)
            table[h, n1 * 128:(n1 + 1) * 128, :] = jnp.concatenate([re_hi, im_hi, re_lo, im_lo], axis=1)

    for copy in index_copies:
        copy.wait()
    shot_lane = shot_idx[...]
    slot_lane = slot_idx[...]
    station_lane = station_idx[...].astype(F32)
    slot_rows[...] = hot(iota((SLOTS, TDEV), 0) == slot_lane)
    shots = hot(iota((16, TDEV), 0) == shot_lane)
    slots = slot_rows[...]
    shot_count = jnp.sum(shots.astype(F32), axis=1, keepdims=True)
    counts = lax.dot_general(shots, slots, NT_DIMS, preferred_element_type=F32).astype(BF16)
    counts_t = lax.dot_general(slots, shots, NT_DIMS, preferred_element_type=F32).astype(BF16)
    slot_count = lax.dot_general(jnp.ones((8, TDEV), BF16), slots, NT_DIMS, preferred_element_type=F32)[0:1, :]
    meta = jnp.zeros((64, NB), F32)
    lane = iota((64, NB), 1)
    for c in range(4):
        named = iota((64, SLOTS), 1) == iota((64, SLOTS), 0) * 4 + c
        meta = jnp.where(lane == c, jnp.sum(jnp.where(named, station_lane, 0.0), axis=1, keepdims=True), meta)
        meta = jnp.where(lane == 4 + c, jnp.sum(jnp.where(named, slot_count, 0.0), axis=1, keepdims=True), meta)
    first_send[:, 4:5, :] = meta.reshape(64, 1, NB)

    sign = 1.0 - 2.0 * (iota((1, HALF), 1) & 1).astype(F32)

    @pl.loop(0, 8)
    def _(c):
        x_copy(c).wait()
        rows = pl.ds(pl.multiple_of(c * 64, 64), 64)
        first, second = xbuf[rows, :HALF], xbuf[rows, HALF:]
        u, v = first + second, first - second
        nyquist = jnp.sum(u * sign, axis=1, keepdims=True) * (1.0 / HALF)
        rest = u - nyquist * sign
        energy = jnp.sum(rest * rest + v * v, axis=1, keepdims=True) * 0.5
        mean = jnp.sum(u, axis=1, keepdims=True)
        level[rows, :] = jnp.broadcast_to((energy + mean * mean * (1.0 / NT)) * (0.01 * 0.5 / 1024.0), (64, NB))
        uhi[rows, :], ulo[rows, :] = split(u, 2)
        vhi[rows, :], vlo[rows, :] = split(v, 2)

    shot_sums, slot_sums, shot_terms = [None, None], [None, None], [None, None]
    def transform(h, hi, lo, rows):
        full = jnp.dot(hi[rows, :], table[h], preferred_element_type=F32)
        rest = jnp.dot(lo[rows, :], table[h, :, :256], preferred_element_type=F32)
        both = full[:, :256] + (full[:, 256:] + rest)
        spec[rows, h * 256:(h + 1) * 256] = both
        re, im = both[:, :NB], both[:, NB:]
        logs[h, rows, :] = jnp.log(re * re + im * im + level[rows, :])

    def odd_rows(k):
        transform(1, vhi, vlo, pl.ds(k * 64 if isinstance(k, int) else pl.multiple_of(k * 64, 64), 64))

    for part in range(2):
        transform(0, uhi, ulo, pl.ds(part * 256, 256))
    for h in range(2):
        shot_sums[h] = hot_dot(shots, logs[h])
        slot_sums[h] = hot_dot(slot_rows[...], logs[h])
        shot_terms[h] = shot_sums[h] / shot_count
        sums = slot_sums[h] - hot_dot(counts_t, shot_terms[h])
        if h == 0:
            first_send[:, 0:4, :] = sums.reshape(64, 4, NB)
            pl.semaphore_wait(barrier, 66)
            exchange(0, five(first_send), five(first_recv), odd_rows)
            part = first_send.at[pl.ds(0, 63), pl.ds(0, 5)]
            pending.append(pltpu.make_async_copy(part, part, a2a_send.at[0]).wait)
        else:
            sum_send[0] = sums
            exchange_rows(1, sum_send.at[0], sum_recv.at[0])

    by_row = jnp.transpose(jnp.concatenate(
        [shot_lane.astype(F32), slot_lane.astype(F32), jnp.zeros((6, TDEV), F32)], axis=0
    ))
    shot_cols[...] = hot(iota((TDEV, 16), 1).astype(F32) == by_row[:, 0:1])
    slot_cols[...] = hot(iota((TDEV, SLOTS), 1).astype(F32) == by_row[:, 1:2])

    part = first_recv.at[:, pl.ds(0, 5)]
    pltpu.make_async_copy(part, part, a2a_recv.at[0]).wait()
    of_source = hot(lax.shift_right_logical(iota((SLOTS, 64), 0), 2) == iota((SLOTS, 64), 1))
    meta = hot_dot(of_source, first_recv[:, 4:5, :].reshape(64, NB), 2)
    lane, own = iota((SLOTS, NB), 1), iota((SLOTS, NB), 0) & 3
    station = jnp.sum(jnp.where(lane == own, meta, 0.0), axis=1, keepdims=True)
    count = jnp.sum(jnp.where(lane == own + 4, meta, 0.0), axis=1, keepdims=True)
    owner_cols[...] = hot(station == iota((SLOTS, 32), 1).astype(F32))
    owner = owner_cols[...]
    station_count = hot_dot(owner, jnp.broadcast_to(count, (SLOTS, NB)), 2, TN_DIMS)
    terms = [None, None]

    def at_owner(sweep, h):
        if sweep == 0 and h == 0:
            sums = first_recv[:, 0:4, :].reshape(SLOTS, NB)
        else:
            slot = sweep * 2 + h - 1
            arrived(1 if sweep == 0 else 4 + h, sum_recv.at[slot])
            sums = sum_recv[slot]
        terms[h] = hot_dot(owner, sums, 3, TN_DIMS) / station_count
        slot = sweep * 2 + h
        term_send[slot] = hot_dot(owner, terms[h])
        exchange_rows(2 + sweep * 4 + h, term_send.at[slot], term_recv.at[slot])

    def at_source(h):
        arrived(2 + h, term_recv.at[h])
        shot_terms[h] = (shot_sums[h] - hot_dot(counts, term_recv[h])) / shot_count
        sum_send[1 + h] = slot_sums[h] - hot_dot(counts_t, shot_terms[h])
        exchange_rows(4 + h, sum_send.at[1 + h], sum_recv.at[1 + h])

    at_owner(0, 0)
    at_owner(0, 1)
    for c in range(4):
        rows = slice(c * 512, (c + 1) * 512)
        owner_lane = owner_idx[...]
        local_lane = local_idx[...]
        place = (owner_lane & 1) * 1024 + lax.shift_right_logical(local_lane, 4) * 512 + (
            lax.shift_right_logical(owner_lane, 1) & 3) * 128 + lax.shift_right_logical(owner_lane, 3) * 16 + (local_lane & 15)
        cmp_hot[rows, :] = hot(iota((512, TDEV), 0) + c * 512 == place)
    at_source(0)
    at_source(1)
    at_owner(1, 0)
    at_owner(1, 1)

    k0, k1 = iota((256, 256), 0), iota((256, 256), 1)
    order = hot(k1 == 2 * (k0 & 127) + lax.shift_right_logical(k0, 7))

    def ordered(even, odd):
        total = jnp.zeros((even.shape[0], 256), F32)
        for piece in split(jnp.concatenate([even, odd], axis=1), 3):
            total = total + jnp.dot(piece, order, preferred_element_type=F32)
        return total

    shot_buf[...] = ordered(shot_terms[0], shot_terms[1])
    rec_buf[...] = ordered(terms[0], terms[1])
    out_copies = [
        pltpu.make_async_copy(source, target, out_sem.at[i])
        for i, (source, target) in enumerate(((shot_buf, shot_out), (rec_buf, rec_out), (cmp_buf, cmp_out)))
    ]
    out_copies[0].start()
    out_copies[1].start()
    shot_part = [hot_dot(shot_cols[...], shot_terms[h]) for h in range(2)]
    ones = jnp.ones((8, NB), BF16)
    partial = jnp.zeros((8, TDEV), F32)
    for h in range(2):
        arrived(6 + h, term_recv.at[2 + h])
        root = jnp.exp(0.5 * (shot_part[h] + hot_dot(slot_cols[...], term_recv[2 + h])))
        roots[h] = root
        for piece in split(root * root, 3):
            partial = partial + lax.dot_general(ones, piece, NT_DIMS, preferred_element_type=F32)
    q_send[...] = partial[0:1, :]
    q_recv[band] = partial[0:1, :]
    q_copies = []
    for p in (2, 1, 3):
        copy = pltpu.make_async_remote_copy(
            src_ref=q_send, dst_ref=q_recv.at[band], send_sem=q_ssem.at[p - 1], recv_sem=q_rsem.at[p - 1],
            device_id={"freq": lax.rem(band + p, 4)},
        )
        copy.start()
        q_copies.append(copy)
    for copy in q_copies:
        copy.wait()
    total = (q_recv[0] + q_recv[1]) + (q_recv[2] + q_recv[3])
    floor = jnp.transpose(jnp.broadcast_to(total, (8, TDEV)))[:, 0:1] * (0.3 / 1024.0)
    floor = jnp.broadcast_to(floor, (TDEV, NB))
    def deconvolve(h):
        root = roots[h]
        wiener = root / (root * root + floor)
        for c in range(2):
            cols = slice((2 * h + c) * NB, (2 * h + c + 1) * NB)
            spec[:, cols] = wiener * spec[:, cols]


    sibling = {"trace": me + 1 - 2 * core}

    def at_x(step):
        return {"trace": z * 8 + lax.rem(x + step, 4) * 2 + core}

    def at_z(step):
        return {"trace": lax.rem(z + step, 8) * 8 + x * 2 + core}

    def send(src, dst, sems, at, to):
        return pltpu.make_async_remote_copy(
            src_ref=src, dst_ref=dst, send_sem=sems.at[(0, *at)], recv_sem=sems.at[(1, *at)], device_id=to
        )

    pieces = ((0, 0, 1), (1, 0, 2), (0, 1, 1), (2, 0, 2), (3, 0, 1), (3, 1, 1))

    def stack(i, of_core):
        g, first, size = pieces[i]
        rows = pl.ds(pl.multiple_of(of_core * 1024 + first * 512, 512), size * 512)
        parts = jnp.concatenate(split(spec[:, g * NB:(g + 1) * NB], 2), axis=1)
        full = jnp.dot(cmp_hot[rows, :], parts, preferred_element_type=F32)
        value = (full[:, :NB] + full[:, NB:]).reshape(size, 4, 8, 16, NB)
        dense[g, of_core, first:first + size] = value

    def step0(i):
        g, first, size = pieces[i]
        half = pl.ds(first, size)
        return send(dense.at[g, 1 - core, half], rs0.at[g, half], rs0_sem, (i,), sibling)

    def begin(i):
        stack(i, 1 - core)
        step0(i).start()
        stack(i, core)

    def join(i):
        g, first, size = pieces[i]
        step0(i).wait_recv()
        dense[g, core, first:first + size] = dense[g, core, first:first + size] + rs0[g, first:first + size]

    def far(g, first, size, step, d):
        if size == 2:
            return dense.at[g, core, d, lax.rem(x + step, 4)]
        return dense.at[g, core, first, lax.rem(x + step, 4), pl.ds(4 * d, 4)]

    def step1(i, d):
        g, first, size = pieces[i]
        dst = rs1.at[g, d] if size == 2 else rs1.at[g, d, pl.ds(4 * first, 4)]
        return send(far(g, first, size, 2, d), dst, rs1_sem, (i, d), at_x(1 + 2 * d))

    def step2(i, d):
        g, first, size = pieces[i]
        half = pl.ds(first, size)
        return send(
            dense.at[g, core, half, lax.rem(x + 1 + 2 * d, 4)], rs2.at[g, d, half], rs2_sem, (i, d), at_x(1 + 2 * d)
        )

    def after0(i):
        join(i)
        for d in range(2):
            step1(i, d).start()

    def after1(i):
        g, first, size = pieces[i]
        for d in range(2):
            step1(i, d).wait_recv()
            there = lax.rem(x + 1 + 2 * d, 4)
            if size == 2:
                dense[g, core, d, there] = dense[g, core, d, there] + rs1[g, d]
            else:
                rows = slice(4 * d, 4 * d + 4)
                dense[g, core, first, there, rows] = dense[g, core, first, there, rows] + rs1[g, d, 4 * first:4 * first + 4]
            step2(i, d).start()

    def step3(i, p):
        g, first, size = pieces[i]
        half = pl.ds(first, size)
        return send(
            dense.at[g, core, half, x, lax.rem(z + p, 8)], rs3.at[g, z, half], rs3_sem, (i,), at_z(p)
        )

    def after2(i):
        g, first, size = pieces[i]
        for d in range(2):
            step2(i, d).wait_recv()
        last = first + size
        dense[g, core, first:last, x] = dense[g, core, first:last, x] + (rs2[g, 0, first:last] + rs2[g, 1, first:last])
        for p in (4, 3, 5, 2, 6, 1, 7):
            step3(i, p).start()
        rs3[g, z, first:last] = dense[g, core, first:last, x, z]

    def step3_bytes(i, way):
        g, first, size = pieces[i]
        part = rs3.at[g, pl.ds(0, 7), pl.ds(first, size)]
        return pltpu.make_async_copy(part, part, rs3_sem.at[way, i])

    def after3(i):
        g, first, size = pieces[i]
        last = first + size
        step3_bytes(i, 1).wait()
        total = rs3[g, 0, first:last]
        for source in range(1, 8):
            total = total + rs3[g, source, first:last]
        stacked[g, 16 * first:16 * last, :] = 0.25 * total.reshape(16 * size, NB)

    def round_z(flow, step):
        there = lax.rem(z + 4 - step, 8) if flow == 0 else lax.rem(z + 5 + step, 8)
        return send(
            dense.at[1, core, :, :, there], rsz.at[flow, step], rsz_sem, (flow, step), at_z(1 if flow == 0 else 7)
        )

    def x_last(p):
        return send(zsum.at[:, lax.rem(x + p, 4)], rsx.at[x], rsx_sem, (p - 1,), at_x(p))

    def side0():
        join(1)
        round_z(0, 0).start()
        round_z(1, 0).start()

    def side(step):
        for flow in range(2):
            if step <= 3:
                round_z(flow, step - 1).wait_recv()
                there = lax.rem(z + 4 - step, 8) if flow == 0 else lax.rem(z + 5 + step, 8)
                dense[1, core, :, :, there] = dense[1, core, :, :, there] + rsz[flow, step - 1]
                if flow == 0 or step < 3:
                    round_z(flow, step).start()

    def side4():
        round_z(0, 3).wait_recv()
        zsum[...] = dense[1, core, :, :, z] + rsz[0, 3]
        for p in (2, 1, 3):
            x_last(p).start()
        rsx[x] = zsum[:, x]

    def side5():
        for p in range(1, 4):
            x_last(p).wait_recv()
        stacked[1] = 0.25 * ((rsx[0] + rsx[1]) + (rsx[2] + rsx[3])).reshape(32, NB)

    deconvolve(0)
    begin(0)
    begin(1)
    after0(0)
    begin(2)
    side0()
    deconvolve(1)
    after0(2)
    begin(3)
    after1(0)
    begin(4)
    after0(3)
    after1(2)
    side(1)
    begin(5)
    after0(4)
    after2(0)
    after1(3)
    after0(5)
    after2(2)
    side(2)
    after1(4)
    after3(0)
    after1(5)
    after2(3)
    side(3)
    after2(4)
    after3(2)
    after3(3)
    cmp_buf[:, 0, :] = ordered(stacked[0], stacked[2])
    after2(5)
    side4()
    for i in range(6):
        pending.append(step0(i).wait_send)
    for i in (0, 2, 3, 4, 5):
        for d in range(2):
            pending.append(step1(i, d).wait_send)
            pending.append(step2(i, d).wait_send)
        if i < 5:
            pending.append(step3_bytes(i, 0).wait)
    for step in range(4):
        pending.append(round_z(0, step).wait_send)
    for step in range(3):
        pending.append(round_z(1, step).wait_send)
    for p in range(1, 4):
        pending.append(x_last(p).wait_send)
    for wait in pending:
        wait()
    after3(4)
    side5()
    after3(5)
    cmp_buf[:, 1, :] = ordered(stacked[1], stacked[3])
    out_copies[2].start()
    step3_bytes(5, 0).wait()
    for copy in out_copies:
        copy.wait()


def copy_kernel(a, b, c, x, y, z, p, q, r, sems):
    triples = ((a, p, x), (b, q, y), (c, r, z))
    reads = [pltpu.make_async_copy(s, m, sems.at[0, i]) for i, (s, m, t) in enumerate(triples)]
    writes = [pltpu.make_async_copy(m, t, sems.at[1, i]) for i, (s, m, t) in enumerate(triples)]
    for copy in reads:
        copy.start()
    for read, write in zip(reads, writes):
        read.wait()
        write.start()
    for copy in writes:
        copy.wait()


def shards(low_tab, high_tab, traces, shot_local, rec_slot, slot_station, cmp_owner, cmp_local):
    vmem = pltpu.VMEM
    dma = pltpu.SemaphoreType.DMA
    i32 = jnp.int32
    outs = (
        jax.ShapeDtypeStruct((16, 256), F32),
        jax.ShapeDtypeStruct((32, 256), F32),
        jax.ShapeDtypeStruct((32, 2, 256), F32),
    )
    results = pl.pallas_call(
        kernel,
        out_shape=outs,
        in_specs=[pl.BlockSpec(memory_space=pl.ANY)] * 8,
        out_specs=(pl.BlockSpec(memory_space=pl.ANY),) * 3,
        scratch_shapes=[
            vmem((TDEV, NT), F32), vmem((2, 128, 256), F32), vmem((2, 8, 256), F32), vmem((2, HALF, 512), BF16),
            vmem((TDEV, HALF), BF16), vmem((TDEV, HALF), BF16), vmem((TDEV, HALF), BF16), vmem((TDEV, HALF), BF16),
            vmem((TDEV, NB), F32), vmem((TDEV, 512), F32), vmem((2, TDEV, NB), F32), vmem((2, TDEV, NB), F32),
            vmem((1, TDEV), i32), vmem((1, TDEV), i32), vmem((1, SLOTS), i32), vmem((1, TDEV), i32), vmem((1, TDEV), i32),
            vmem((SLOTS, TDEV), BF16), vmem((TDEV, SLOTS), BF16), vmem((TDEV, 16), BF16),
            vmem((2048, TDEV), BF16), vmem((SLOTS, 32), BF16),
            vmem((64, 8, NB), F32), vmem((64, 8, NB), F32),
            vmem((3, SLOTS, NB), F32), vmem((3, SLOTS, NB), F32), vmem((4, SLOTS, NB), F32), vmem((4, SLOTS, NB), F32),
            vmem((1, TDEV), F32), vmem((4, 1, TDEV), F32),
            vmem((4, 2, 2, 4, 8, 16, NB), F32), vmem((4, 2, 4, 8, 16, NB), F32), vmem((4, 2, 8, 16, NB), F32),
            vmem((4, 2, 2, 8, 16, NB), F32), vmem((4, 8, 2, 16, NB), F32),
            vmem((2, 4, 2, 4, 16, NB), F32), vmem((2, 4, 16, NB), F32), vmem((4, 2, 16, NB), F32), vmem((4, 32, NB), F32),
            vmem((16, 256), F32), vmem((32, 256), F32), vmem((32, 2, 256), F32),
            dma((8,)), dma((2,)), dma((5,)), dma((8,)), dma((8,)), dma((3,)), dma((3,)),
            dma((2, 6)), dma((2, 6, 2)), dma((2, 6, 2)), dma((2, 6)), dma((2, 2, 4)), dma((2, 3)), dma((3,)),
        ],
        compiler_params=pltpu.CompilerParams(
            collective_id=0, has_side_effects=True, vmem_limit_bytes=56 * 1024 * 1024
        ),
    )(
        traces, shot_local, rec_slot, slot_station, cmp_owner.reshape(1, TDEV), cmp_local.reshape(1, TDEV),
        low_tab, high_tab,
    )
    return tuple(pl.pallas_call(
        copy_kernel,
        out_shape=outs,
        in_specs=[pl.BlockSpec(memory_space=pl.ANY)] * 3,
        out_specs=(pl.BlockSpec(memory_space=pl.ANY),) * 3,
        scratch_shapes=[vmem((16, 256), F32), vmem((32, 256), F32), vmem((32, 2, 256), F32), dma((2, 3))],
        compiler_params=pltpu.CompilerParams(vmem_limit_bytes=56 * 1024 * 1024),
    )(*results))


def solution(mesh):
    low, high = twiddles()
    body = jax.shard_map(
        shards,
        mesh=mesh,
        in_specs=(
            P(), P(),
            P("trace", None),
            P("trace", None),
            P("trace", None),
            P("trace", None),
            P("trace", None),
            P("trace"),
        ),
        out_specs=(P("trace", "freq"), P("trace", "freq"), P("trace", None, "freq")),
        check_vma=False,
    )
    return functools.partial(body, low, high)
```

```python
import functools

import jax
import jax.numpy as jnp
import numpy as np
from jax import lax
from jax.experimental import pallas as pl
from jax.experimental.pallas import tpu as pltpu
from jax.sharding import PartitionSpec as P

NT = 2048
HALF = 1024
NB = 128
TDEV = 512
SLOTS = 256
F32 = jnp.float32
BF16 = jnp.bfloat16
NT_DIMS = (((1,), (1,)), ((), ()))
TN_DIMS = (((0,), (0,)), ((), ()))


def twiddles():
    bins = np.arange(4)[:, None, None] * 256 + np.arange(2)[None, :, None] + 2 * np.arange(NB)[None, None, :]
    low = -2.0 * np.pi * ((np.arange(128)[:, None] * bins[:, :, None, :]) % NT) / NT
    high = -2.0 * np.pi * ((128 * np.arange(8)[:, None] * bins[:, :, None, :]) % NT) / NT
    norm = NT**-0.5
    low = np.concatenate([np.cos(low), np.sin(low)], axis=-1) * norm
    high = np.concatenate([np.cos(high), np.sin(high)], axis=-1)
    return low.astype(np.float32), high.astype(np.float32)


def split(x, parts):
    out = []
    for i in range(parts):
        piece = x.astype(BF16)
        out.append(piece)
        if i + 1 < parts:
            x = x - piece.astype(F32)
    return out


def hot_dot(hot, x, parts=3, dims=(((1,), (0,)), ((), ()))):
    n = x.shape[1]
    full = lax.dot_general(hot, jnp.concatenate(split(x, parts), axis=1), dims, preferred_element_type=F32)
    total = full[:, :n]
    for i in range(1, parts):
        total = total + full[:, i * n:(i + 1) * n]
    return total


def iota(shape, axis):
    return lax.broadcasted_iota(jnp.int32, shape, axis)


def hot(condition):
    return jnp.where(condition, 1.0, 0.0).astype(BF16)


def kernel(
    traces, shot_in, slot_in, station_in, owner_in, local_in, low_tab, high_tab,
    shot_out, rec_out, cmp_out,
    xbuf, low, high, table, uhi, ulo, vhi, vlo, level, spec, logs, roots,
    shot_idx, slot_idx, station_idx, owner_idx, local_idx,
    slot_rows, slot_cols, shot_cols, cmp_hot, owner_cols,
    first_send, first_recv, sum_send, sum_recv, term_send, term_recv, q_send, q_recv,
    dense, rs0, rs1, rs2, rs3, rsz, zsum, rsx, stacked, shot_buf, rec_buf, cmp_buf,
    x_sem, tab_sem, idx_sem, a2a_send, a2a_recv, q_ssem, q_rsem, rs0_sem, rs1_sem, rs2_sem, rs3_sem, rsz_sem, rsx_sem, out_sem,
):
    me = lax.axis_index("trace")
    band = lax.axis_index("freq")
    z = lax.div(me, 8)
    x = lax.rem(lax.div(me, 2), 4)
    core = lax.rem(me, 2)
    pending = []
    places = [lax.rem(x + dx, 4) * 2 + lax.rem(core + dc, 2) for dx in (2, 1, 3, 0) for dc in (1, 0)]

    def x_copy(c):
        rows = pl.ds(c * 64, 64)
        return pltpu.make_async_copy(traces.at[rows], xbuf.at[rows], x_sem.at[c])

    low_copy = pltpu.make_async_copy(low_tab.at[band], low, tab_sem.at[0])
    high_copy = pltpu.make_async_copy(high_tab.at[band], high, tab_sem.at[1])
    index_copies = [
        pltpu.make_async_copy(source, target, idx_sem.at[i])
        for i, (source, target) in enumerate((
            (shot_in, shot_idx), (slot_in, slot_idx), (station_in, station_idx), (owner_in, owner_idx), (local_in, local_idx),
        ))
    ]
    low_copy.start()
    high_copy.start()
    for c in range(8):
        x_copy(c).start()
    for copy in index_copies:
        copy.start()

    barrier = pltpu.get_barrier_semaphore()

    @pl.loop(1, 64)
    def _(p):
        pl.semaphore_signal(barrier, inc=1, device_id={"trace": lax.rem(me + p, 64)})

    for p in range(1, 4):
        pl.semaphore_signal(barrier, inc=1, device_id={"freq": lax.rem(band + p, 4)})

    def exchange(leg, source_of, target, beside=None):
        sems = dict(send_sem=a2a_send.at[leg], recv_sem=a2a_recv.at[leg])

        def put(other):
            pltpu.make_async_remote_copy(
                src_ref=source_of(other), dst_ref=target(me), device_id={"trace": other}, **sems
            ).start()

        @pl.loop(0, 7)
        def _(k):
            side = 1 - 2 * lax.rem(k, 2)
            there = lax.rem(z + 12 + side * lax.div(k + 1, 2), 8) * 8
            for place in places:
                put(there + place)
            if beside is not None:
                beside(k)

        for place in places[:7]:
            put(z * 8 + place)
        pltpu.make_async_copy(source_of(me), target(me), a2a_recv.at[leg]).start()
        if beside is not None:
            beside(7)

    def four(ref):
        return lambda d: ref.at[pl.ds(pl.multiple_of(d * 4, 4), 4)]

    def five(ref):
        return lambda d: ref.at[d, pl.ds(0, 5)]

    def exchange_rows(leg, source, target):
        exchange(leg, four(source), four(target))
        part = source.at[pl.ds(0, 252)]
        pending.append(pltpu.make_async_copy(part, part, a2a_send.at[leg]).wait)

    def arrived(leg, target):
        pltpu.make_async_copy(target, target, a2a_recv.at[leg]).wait()

    low_copy.wait()
    high_copy.wait()
    for h in range(2):
        low_re, low_im = low[h, :, :NB], low[h, :, NB:]
        for n1 in range(8):
            high_re, high_im = high[h, n1:n1 + 1, :NB], high[h, n1:n1 + 1, NB:]
            re_hi, re_lo = split(low_re * high_re - low_im * high_im, 2)
            im_hi, im_lo = split(low_re * high_im + low_im * high_re, 2)
            table[h, n1 * 128:(n1 + 1) * 128, :] = jnp.concatenate([re_hi, im_hi, re_lo, im_lo], axis=1)

    for copy in index_copies:
        copy.wait()
    shot_lane = shot_idx[...]
    slot_lane = slot_idx[...]
    station_lane = station_idx[...].astype(F32)
    slot_rows[...] = hot(iota((SLOTS, TDEV), 0) == slot_lane)
    shots = hot(iota((16, TDEV), 0) == shot_lane)
    slots = slot_rows[...]
    shot_count = jnp.sum(shots.astype(F32), axis=1, keepdims=True)
    counts = lax.dot_general(shots, slots, NT_DIMS, preferred_element_type=F32).astype(BF16)
    counts_t = lax.dot_general(slots, shots, NT_DIMS, preferred_element_type=F32).astype(BF16)
    slot_count = lax.dot_general(jnp.ones((8, TDEV), BF16), slots, NT_DIMS, preferred_element_type=F32)[0:1, :]
    meta = jnp.zeros((64, NB), F32)
    lane = iota((64, NB), 1)
    for c in range(4):
        named = iota((64, SLOTS), 1) == iota((64, SLOTS), 0) * 4 + c
        meta = jnp.where(lane == c, jnp.sum(jnp.where(named, station_lane, 0.0), axis=1, keepdims=True), meta)
        meta = jnp.where(lane == 4 + c, jnp.sum(jnp.where(named, slot_count, 0.0), axis=1, keepdims=True), meta)
    first_send[:, 4:5, :] = meta.reshape(64, 1, NB)

    sign = 1.0 - 2.0 * (iota((1, HALF), 1) & 1).astype(F32)

    @pl.loop(0, 8)
    def _(c):
        x_copy(c).wait()
        rows = pl.ds(pl.multiple_of(c * 64, 64), 64)
        first, second = xbuf[rows, :HALF], xbuf[rows, HALF:]
        u, v = first + second, first - second
        nyquist = jnp.sum(u * sign, axis=1, keepdims=True) * (1.0 / HALF)
        rest = u - nyquist * sign
        energy = jnp.sum(rest * rest + v * v, axis=1, keepdims=True) * 0.5
        mean = jnp.sum(u, axis=1, keepdims=True)
        level[rows, :] = jnp.broadcast_to((energy + mean * mean * (1.0 / NT)) * (0.01 * 0.5 / 1024.0), (64, NB))
        uhi[rows, :], ulo[rows, :] = split(u, 2)
        vhi[rows, :], vlo[rows, :] = split(v, 2)

    shot_sums, slot_sums, shot_terms = [None, None], [None, None], [None, None]
    def transform(h, hi, lo, rows):
        full = jnp.dot(hi[rows, :], table[h], preferred_element_type=F32)
        rest = jnp.dot(lo[rows, :], table[h, :, :256], preferred_element_type=F32)
        both = full[:, :256] + (full[:, 256:] + rest)
        spec[rows, h * 256:(h + 1) * 256] = both
        re, im = both[:, :NB], both[:, NB:]
        logs[h, rows, :] = jnp.log(re * re + im * im + level[rows, :])

    def odd_rows(k):
        transform(1, vhi, vlo, pl.ds(k * 64 if isinstance(k, int) else pl.multiple_of(k * 64, 64), 64))

    for part in range(2):
        transform(0, uhi, ulo, pl.ds(part * 256, 256))
    for h in range(2):
        shot_sums[h] = hot_dot(shots, logs[h])
        slot_sums[h] = hot_dot(slot_rows[...], logs[h])
        shot_terms[h] = shot_sums[h] / shot_count
        sums = slot_sums[h] - hot_dot(counts_t, shot_terms[h])
        if h == 0:
            first_send[:, 0:4, :] = sums.reshape(64, 4, NB)
            pl.semaphore_wait(barrier, 66)
            exchange(0, five(first_send), five(first_recv), odd_rows)
            part = first_send.at[pl.ds(0, 63), pl.ds(0, 5)]
            pending.append(pltpu.make_async_copy(part, part, a2a_send.at[0]).wait)
        else:
            sum_send[0] = sums
            exchange_rows(1, sum_send.at[0], sum_recv.at[0])

    by_row = jnp.transpose(jnp.concatenate(
        [shot_lane.astype(F32), slot_lane.astype(F32), jnp.zeros((6, TDEV), F32)], axis=0
    ))
    shot_cols[...] = hot(iota((TDEV, 16), 1).astype(F32) == by_row[:, 0:1])
    slot_cols[...] = hot(iota((TDEV, SLOTS), 1).astype(F32) == by_row[:, 1:2])

    part = first_recv.at[:, pl.ds(0, 5)]
    pltpu.make_async_copy(part, part, a2a_recv.at[0]).wait()
    of_source = hot(lax.shift_right_logical(iota((SLOTS, 64), 0), 2) == iota((SLOTS, 64), 1))
    meta = hot_dot(of_source, first_recv[:, 4:5, :].reshape(64, NB), 2)
    lane, own = iota((SLOTS, NB), 1), iota((SLOTS, NB), 0) & 3
    station = jnp.sum(jnp.where(lane == own, meta, 0.0), axis=1, keepdims=True)
    count = jnp.sum(jnp.where(lane == own + 4, meta, 0.0), axis=1, keepdims=True)
    owner_cols[...] = hot(station == iota((SLOTS, 32), 1).astype(F32))
    owner = owner_cols[...]
    station_count = hot_dot(owner, jnp.broadcast_to(count, (SLOTS, NB)), 2, TN_DIMS)
    terms = [None, None]

    def at_owner(sweep, h):
        if sweep == 0 and h == 0:
            sums = first_recv[:, 0:4, :].reshape(SLOTS, NB)
        else:
            slot = sweep * 2 + h - 1
            arrived(1 if sweep == 0 else 4 + h, sum_recv.at[slot])
            sums = sum_recv[slot]
        terms[h] = hot_dot(owner, sums, 3, TN_DIMS) / station_count
        slot = sweep * 2 + h
        term_send[slot] = hot_dot(owner, terms[h])
        exchange_rows(2 + sweep * 4 + h, term_send.at[slot], term_recv.at[slot])

    def at_source(h):
        arrived(2 + h, term_recv.at[h])
        shot_terms[h] = (shot_sums[h] - hot_dot(counts, term_recv[h])) / shot_count
        sum_send[1 + h] = slot_sums[h] - hot_dot(counts_t, shot_terms[h])
        exchange_rows(4 + h, sum_send.at[1 + h], sum_recv.at[1 + h])

    at_owner(0, 0)
    at_owner(0, 1)
    for c in range(4):
        rows = slice(c * 512, (c + 1) * 512)
        owner_lane = owner_idx[...]
        local_lane = local_idx[...]
        place = (owner_lane & 1) * 1024 + lax.shift_right_logical(local_lane, 4) * 512 + (
            lax.shift_right_logical(owner_lane, 1) & 3) * 128 + lax.shift_right_logical(owner_lane, 3) * 16 + (local_lane & 15)
        cmp_hot[rows, :] = hot(iota((512, TDEV), 0) + c * 512 == place)
    at_source(0)
    at_source(1)
    at_owner(1, 0)
    at_owner(1, 1)

    k0, k1 = iota((256, 256), 0), iota((256, 256), 1)
    order = hot(k1 == 2 * (k0 & 127) + lax.shift_right_logical(k0, 7))

    def ordered(even, odd):
        total = jnp.zeros((even.shape[0], 256), F32)
        for piece in split(jnp.concatenate([even, odd], axis=1), 3):
            total = total + jnp.dot(piece, order, preferred_element_type=F32)
        return total

    shot_buf[...] = ordered(shot_terms[0], shot_terms[1])
    rec_buf[...] = ordered(terms[0], terms[1])
    out_copies = [
        pltpu.make_async_copy(source, target, out_sem.at[i])
        for i, (source, target) in enumerate(((shot_buf, shot_out), (rec_buf, rec_out), (cmp_buf, cmp_out)))
    ]
    out_copies[0].start()
    out_copies[1].start()
    shot_part = [hot_dot(shot_cols[...], shot_terms[h]) for h in range(2)]
    ones = jnp.ones((8, NB), BF16)
    partial = jnp.zeros((8, TDEV), F32)
    for h in range(2):
        arrived(6 + h, term_recv.at[2 + h])
        root = jnp.exp(0.5 * (shot_part[h] + hot_dot(slot_cols[...], term_recv[2 + h])))
        roots[h] = root
        for piece in split(root * root, 3):
            partial = partial + lax.dot_general(ones, piece, NT_DIMS, preferred_element_type=F32)
    q_send[...] = partial[0:1, :]
    q_recv[band] = partial[0:1, :]
    q_copies = []
    for p in (2, 1, 3):
        copy = pltpu.make_async_remote_copy(
            src_ref=q_send, dst_ref=q_recv.at[band], send_sem=q_ssem.at[p - 1], recv_sem=q_rsem.at[p - 1],
            device_id={"freq": lax.rem(band + p, 4)},
        )
        copy.start()
        q_copies.append(copy)
    for copy in q_copies:
        copy.wait()
    total = (q_recv[0] + q_recv[1]) + (q_recv[2] + q_recv[3])
    floor = jnp.transpose(jnp.broadcast_to(total, (8, TDEV)))[:, 0:1] * (0.3 / 1024.0)
    floor = jnp.broadcast_to(floor, (TDEV, NB))
    def deconvolve(h):
        root = roots[h]
        wiener = root / (root * root + floor)
        for c in range(2):
            cols = slice((2 * h + c) * NB, (2 * h + c + 1) * NB)
            spec[:, cols] = wiener * spec[:, cols]


    sibling = {"trace": me + 1 - 2 * core}

    def at_x(step):
        return {"trace": z * 8 + lax.rem(x + step, 4) * 2 + core}

    def at_z(step):
        return {"trace": lax.rem(z + step, 8) * 8 + x * 2 + core}

    def send(src, dst, sems, at, to):
        return pltpu.make_async_remote_copy(
            src_ref=src, dst_ref=dst, send_sem=sems.at[(0, *at)], recv_sem=sems.at[(1, *at)], device_id=to
        )

    pieces = ((0, 0, 1), (1, 0, 2), (0, 1, 1), (2, 0, 2), (3, 0, 1), (3, 1, 1))

    def stack(i, of_core):
        g, first, size = pieces[i]
        rows = pl.ds(pl.multiple_of(of_core * 1024 + first * 512, 512), size * 512)
        parts = jnp.concatenate(split(spec[:, g * NB:(g + 1) * NB], 2), axis=1)
        full = jnp.dot(cmp_hot[rows, :], parts, preferred_element_type=F32)
        value = (full[:, :NB] + full[:, NB:]).reshape(size, 4, 8, 16, NB)
        dense[g, of_core, first:first + size] = value

    def step0(i):
        g, first, size = pieces[i]
        half = pl.ds(first, size)
        return send(dense.at[g, 1 - core, half], rs0.at[g, half], rs0_sem, (i,), sibling)

    def begin(i):
        stack(i, 1 - core)
        step0(i).start()
        stack(i, core)

    def join(i):
        g, first, size = pieces[i]
        step0(i).wait_recv()
        dense[g, core, first:first + size] = dense[g, core, first:first + size] + rs0[g, first:first + size]

    def far(g, first, size, step, d):
        if size == 2:
            return dense.at[g, core, d, lax.rem(x + step, 4)]
        return dense.at[g, core, first, lax.rem(x + step, 4), pl.ds(4 * d, 4)]

    def step1(i, d):
        g, first, size = pieces[i]
        dst = rs1.at[g, d] if size == 2 else rs1.at[g, d, pl.ds(4 * first, 4)]
        return send(far(g, first, size, 2, d), dst, rs1_sem, (i, d), at_x(1 + 2 * d))

    def step2(i, d):
        g, first, size = pieces[i]
        half = pl.ds(first, size)
        return send(
            dense.at[g, core, half, lax.rem(x + 1 + 2 * d, 4)], rs2.at[g, d, half], rs2_sem, (i, d), at_x(1 + 2 * d)
        )

    def after0(i):
        join(i)
        for d in range(2):
            step1(i, d).start()

    def after1(i):
        g, first, size = pieces[i]
        for d in range(2):
            step1(i, d).wait_recv()
            there = lax.rem(x + 1 + 2 * d, 4)
            if size == 2:
                dense[g, core, d, there] = dense[g, core, d, there] + rs1[g, d]
            else:
                rows = slice(4 * d, 4 * d + 4)
                dense[g, core, first, there, rows] = dense[g, core, first, there, rows] + rs1[g, d, 4 * first:4 * first + 4]
            step2(i, d).start()

    def step3(i, p):
        g, first, size = pieces[i]
        half = pl.ds(first, size)
        return send(
            dense.at[g, core, half, x, lax.rem(z + p, 8)], rs3.at[g, z, half], rs3_sem, (i,), at_z(p)
        )

    def after2(i):
        g, first, size = pieces[i]
        for d in range(2):
            step2(i, d).wait_recv()
        last = first + size
        dense[g, core, first:last, x] = dense[g, core, first:last, x] + (rs2[g, 0, first:last] + rs2[g, 1, first:last])
        for p in (4, 3, 5, 2, 6, 1, 7):
            step3(i, p).start()
        rs3[g, z, first:last] = dense[g, core, first:last, x, z]

    def step3_bytes(i, way):
        g, first, size = pieces[i]
        part = rs3.at[g, pl.ds(0, 7), pl.ds(first, size)]
        return pltpu.make_async_copy(part, part, rs3_sem.at[way, i])

    def after3(i):
        g, first, size = pieces[i]
        last = first + size
        step3_bytes(i, 1).wait()
        total = rs3[g, 0, first:last]
        for source in range(1, 8):
            total = total + rs3[g, source, first:last]
        stacked[g, 16 * first:16 * last, :] = 0.25 * total.reshape(16 * size, NB)

    def round_z(flow, step):
        there = lax.rem(z + 4 - step, 8) if flow == 0 else lax.rem(z + 5 + step, 8)
        return send(
            dense.at[1, core, :, :, there], rsz.at[flow, step], rsz_sem, (flow, step), at_z(1 if flow == 0 else 7)
        )

    def x_last(p):
        return send(zsum.at[:, lax.rem(x + p, 4)], rsx.at[x], rsx_sem, (p - 1,), at_x(p))

    def side0():
        join(1)
        round_z(0, 0).start()
        round_z(1, 0).start()

    def side(step):
        for flow in range(2):
            if step <= 3:
                round_z(flow, step - 1).wait_recv()
                there = lax.rem(z + 4 - step, 8) if flow == 0 else lax.rem(z + 5 + step, 8)
                dense[1, core, :, :, there] = dense[1, core, :, :, there] + rsz[flow, step - 1]
                if flow == 0 or step < 3:
                    round_z(flow, step).start()

    def side4():
        round_z(0, 3).wait_recv()
        zsum[...] = dense[1, core, :, :, z] + rsz[0, 3]
        for p in (2, 1, 3):
            x_last(p).start()
        rsx[x] = zsum[:, x]

    def side5():
        for p in range(1, 4):
            x_last(p).wait_recv()
        stacked[1] = 0.25 * ((rsx[0] + rsx[1]) + (rsx[2] + rsx[3])).reshape(32, NB)

    deconvolve(0)
    begin(0)
    begin(1)
    after0(0)
    begin(2)
    side0()
    deconvolve(1)
    after0(2)
    begin(3)
    after1(0)
    begin(4)
    after0(3)
    after1(2)
    side(1)
    begin(5)
    after0(4)
    after2(0)
    after1(3)
    after0(5)
    after2(2)
    after1(4)
    side(2)
    after3(0)
    after1(5)
    after2(3)
    side(3)
    after2(4)
    after3(2)
    after3(3)
    cmp_buf[:, 0, :] = ordered(stacked[0], stacked[2])
    after2(5)
    side4()
    for i in range(6):
        pending.append(step0(i).wait_send)
    for i in (0, 2, 3, 4, 5):
        for d in range(2):
            pending.append(step1(i, d).wait_send)
            pending.append(step2(i, d).wait_send)
        if i < 5:
            pending.append(step3_bytes(i, 0).wait)
    for step in range(4):
        pending.append(round_z(0, step).wait_send)
    for step in range(3):
        pending.append(round_z(1, step).wait_send)
    for p in range(1, 4):
        pending.append(x_last(p).wait_send)
    for wait in pending:
        wait()
    after3(4)
    side5()
    after3(5)
    cmp_buf[:, 1, :] = ordered(stacked[1], stacked[3])
    out_copies[2].start()
    step3_bytes(5, 0).wait()
    for copy in out_copies:
        copy.wait()


def copy_kernel(a, b, c, x, y, z, p, q, r, sems):
    triples = ((a, p, x), (b, q, y), (c, r, z))
    reads = [pltpu.make_async_copy(s, m, sems.at[0, i]) for i, (s, m, t) in enumerate(triples)]
    writes = [pltpu.make_async_copy(m, t, sems.at[1, i]) for i, (s, m, t) in enumerate(triples)]
    for copy in reads:
        copy.start()
    for read, write in zip(reads, writes):
        read.wait()
        write.start()
    for copy in writes:
        copy.wait()


def shards(low_tab, high_tab, traces, shot_local, rec_slot, slot_station, cmp_owner, cmp_local):
    vmem = pltpu.VMEM
    dma = pltpu.SemaphoreType.DMA
    i32 = jnp.int32
    outs = (
        jax.ShapeDtypeStruct((16, 256), F32),
        jax.ShapeDtypeStruct((32, 256), F32),
        jax.ShapeDtypeStruct((32, 2, 256), F32),
    )
    results = pl.pallas_call(
        kernel,
        out_shape=outs,
        in_specs=[pl.BlockSpec(memory_space=pl.ANY)] * 8,
        out_specs=(pl.BlockSpec(memory_space=pl.ANY),) * 3,
        scratch_shapes=[
            vmem((TDEV, NT), F32), vmem((2, 128, 256), F32), vmem((2, 8, 256), F32), vmem((2, HALF, 512), BF16),
            vmem((TDEV, HALF), BF16), vmem((TDEV, HALF), BF16), vmem((TDEV, HALF), BF16), vmem((TDEV, HALF), BF16),
            vmem((TDEV, NB), F32), vmem((TDEV, 512), F32), vmem((2, TDEV, NB), F32), vmem((2, TDEV, NB), F32),
            vmem((1, TDEV), i32), vmem((1, TDEV), i32), vmem((1, SLOTS), i32), vmem((1, TDEV), i32), vmem((1, TDEV), i32),
            vmem((SLOTS, TDEV), BF16), vmem((TDEV, SLOTS), BF16), vmem((TDEV, 16), BF16),
            vmem((2048, TDEV), BF16), vmem((SLOTS, 32), BF16),
            vmem((64, 8, NB), F32), vmem((64, 8, NB), F32),
            vmem((3, SLOTS, NB), F32), vmem((3, SLOTS, NB), F32), vmem((4, SLOTS, NB), F32), vmem((4, SLOTS, NB), F32),
            vmem((1, TDEV), F32), vmem((4, 1, TDEV), F32),
            vmem((4, 2, 2, 4, 8, 16, NB), F32), vmem((4, 2, 4, 8, 16, NB), F32), vmem((4, 2, 8, 16, NB), F32),
            vmem((4, 2, 2, 8, 16, NB), F32), vmem((4, 8, 2, 16, NB), F32),
            vmem((2, 4, 2, 4, 16, NB), F32), vmem((2, 4, 16, NB), F32), vmem((4, 2, 16, NB), F32), vmem((4, 32, NB), F32),
            vmem((16, 256), F32), vmem((32, 256), F32), vmem((32, 2, 256), F32),
            dma((8,)), dma((2,)), dma((5,)), dma((8,)), dma((8,)), dma((3,)), dma((3,)),
            dma((2, 6)), dma((2, 6, 2)), dma((2, 6, 2)), dma((2, 6)), dma((2, 2, 4)), dma((2, 3)), dma((3,)),
        ],
        compiler_params=pltpu.CompilerParams(
            collective_id=0, has_side_effects=True, vmem_limit_bytes=56 * 1024 * 1024
        ),
    )(
        traces, shot_local, rec_slot, slot_station, cmp_owner.reshape(1, TDEV), cmp_local.reshape(1, TDEV),
        low_tab, high_tab,
    )
    return tuple(pl.pallas_call(
        copy_kernel,
        out_shape=outs,
        in_specs=[pl.BlockSpec(memory_space=pl.ANY)] * 3,
        out_specs=(pl.BlockSpec(memory_space=pl.ANY),) * 3,
        scratch_shapes=[vmem((16, 256), F32), vmem((32, 256), F32), vmem((32, 2, 256), F32), dma((2, 3))],
        compiler_params=pltpu.CompilerParams(vmem_limit_bytes=56 * 1024 * 1024),
    )(*results))


def solution(mesh):
    low, high = twiddles()
    body = jax.shard_map(
        shards,
        mesh=mesh,
        in_specs=(
            P(), P(),
            P("trace", None),
            P("trace", None),
            P("trace", None),
            P("trace", None),
            P("trace", None),
            P("trace"),
        ),
        out_specs=(P("trace", "freq"), P("trace", "freq"), P("trace", None, "freq")),
        check_vma=False,
    )
    return functools.partial(body, low, high)
```
